256 devices in a mesh: cache: 16 (over z, y_lo), seq: 8 (over x, core), head: 2 (over y_hi).
Axes of the slice: x: 4, y: 4 (y_hi: 2, y_lo: 2; y = y_hi * 2 + y_lo), z: 8, core: 2. Of those that a mesh axis runs over, the one named last changes fastest.
Arguments:
- hidden: bfloat16 [16, 1024, 4096], P('cache', 'seq', 'head'), may hold values from -6 to 6
- kv_weight: bfloat16 [4096, 2, 1024], P('cache', None, 'head'), may hold values from -0.09375 to 0.09375
- queries: bfloat16 [2, 16, 1024, 4096], P(None, 'cache', 'seq', 'head'), may hold values from -200 to 200, as said below
- kv_pool: bfloat16 [128, 128, 2, 1024], P('cache', None, None, 'head'), may hold values from -6 to 6
- hit_host: int32 [16, 11, 1], replicated, may hold values from 0 to 15; in each aligned block of 11 rows (0 to 10, 11 to 21, ..., all dimensions but the last counted through in order) at most 2 rows name the same one
- hit_page: int32 [16, 11], replicated, may hold values from 0 to 7
- hit_request: int32 [16, 11], replicated, may hold values from 0 to 3
- segment_ids: int32 [16, 1024], P('cache'), may hold values from 0 to 3, never falling along the last dimension, each value on 1 to 512 neighbouring positions
Outputs:
- attended: bfloat16 [2, 16, 1024, 4096], P(None, 'cache', 'seq', 'head')
- kv_new: bfloat16 [16, 1024, 2, 1024], P('cache', 'seq', None, 'head')
The draws below stay inside these ranges and needn't reach their ends.
Inputs may be any that keep to these rules, and one draw needn't show every extreme that they name: queries are real-valued rows of order one to a few tens. `hit_host`: among the 11 hit slots of one span at most 2 name the same host, and some span has exactly 2 slots on one host. `segment_ids`: within a span the ids never fall; each of the 4 requests holds 1 to 512 tokens, one exactly that many.
All inputs are finite; a program needn't handle non-finite values.
Results may differ from the reference program's by a relative error of at most 0.012.
The reference program's roundings to bfloat16 on the way (of `prefix` and `probs_low`) count: a program that leaves them out, or rounds other values in their place, can miss the bound.
Values may be sent and summed in bfloat16 or wider, within the bound.
No kernel may reach another device: no remote copies, remote signals or barrier semaphores. Data moves between devices by JAX's collectives and lax.ppermute only.
A program may use at most 128 MiB of HBM per device.

```python
import math
import jax
import jax.numpy as jnp
import numpy as np
from jax import lax

D = 4096
QH = 32
KVH = 8
HD = 128
PAGE = 128
CAP = 2
HITS = 11
PAGES_DEV = 8
REQS = 4
LAYERS = 2
SPAN = 1024
SPANS = 16
POOL = 128
N_CACHE = 16


def draw_queries(key, part):
    key = jax.random.fold_in(key, 7)
    base = jax.random.truncated_normal(key, -4.0, 4.0, (LAYERS, SPANS, SPAN, QH, HD), jnp.float32)
    return base.reshape(LAYERS, SPANS, SPAN, QH * HD).astype(jnp.bfloat16)


def place_ends(entries, own_key, low, largest):
    longest = entries.shape.index(max(entries.shape))
    spots = []
    for shift in (0, 1):
        where = [jax.random.randint(jax.random.fold_in(own_key, axis), (), 0, length) for axis, length in enumerate(entries.shape)]
        where[longest] = (where[longest] + shift) % entries.shape[longest]
        spots.append(tuple(where))
    return entries.at[spots[0]].set(low).at[spots[1]].set(largest)


def shard_levels(rng, shape, pieces, smallest, high):
    loudness, own = 1.0, jax.random.fold_in(rng, 6)
    for dim, parts in pieces:
        draws = jnp.exp(jax.random.uniform(jax.random.fold_in(own, dim), (parts,), jnp.float32, smallest / len(pieces), high / len(pieces)))
        loudness = loudness * jnp.repeat(draws, shape[dim] // parts).reshape([-1 if axis == dim else 1 for axis in range(len(shape))])
    return loudness


def rank_bounds(number_of, slope):
    portions = [(1 << 20) // math.isqrt(grade ** slope) + 1 for grade in range(1, number_of + 1)]
    scale = 1 + sum(portions) // (1 << 30)
    return np.cumsum(np.array([max(1, weight // scale) for weight in portions]))


def ranked(rng, extent, count, lean):
    grid = rank_bounds(count, lean)
    pick = jax.random.randint(jax.random.fold_in(rng, 1), extent, 0, int(grid[count - 1]))
    standing = jnp.searchsorted(jnp.asarray(grid, jnp.int32), pick, side="right")
    return jax.random.permutation(jax.random.fold_in(rng, 2), count)[standing].astype(jnp.int32)


def split_up(number_of, total, limit, lean):
    weights = [(1 << 20) // math.isqrt(standing ** lean) + 1 for standing in range(2, number_of + 1)]
    surplus, holding = total - limit - (number_of - 1), [1] * (number_of - 1)
    while surplus > 0:
        movable = [i for i in range(number_of - 1) if holding[i] < limit]
        pool, left = sum([weights[i] for i in movable]), surplus
        for i in movable:
            more = min(limit - holding[i], max(1, left * weights[i] // pool), surplus)
            holding[i] = holding[i] + more
            surplus = surplus - more
    return np.array([limit] + holding)


def ragged(stream_key, count, total, most, slope):
    if count == 2:
        one = jax.random.randint(stream_key, (), max(1, total - most), min(most, total - 1) + 1)
        return jnp.stack([one, total - one])
    sizes = jnp.asarray(split_up(count, total, most, slope), jnp.int32)
    pairs = (count - 1) // 2
    donor, receiver = sizes[1:1 + 2 * pairs:2], sizes[2:2 + 2 * pairs:2]
    margin = jnp.minimum(donor - 1, most - receiver)
    shifted = jax.random.randint(jax.random.fold_in(stream_key, 1), (pairs,), 0, 1 << 20) % (margin + 1)
    sizes = sizes.at[1:1 + 2 * pairs:2].set(donor - shifted).at[2:2 + 2 * pairs:2].set(receiver + shifted)
    return sizes[jax.random.permutation(jax.random.fold_in(stream_key, 2), count)]


def shared_out(key, own, number, rows, amount, top, reach, slope):
    order = jax.random.permutation(key, amount)
    packed, usual = portions_of(amount, rows * top, reach, slope, True), portions_of(amount, rows * top, reach, slope, False)
    places = jnp.arange(amount)

    def named(tallies, offset_by):
        used = int((tallies > 0).sum())
        fixed = max(1, used // 4)
        passed = fixed + (places - fixed + offset_by * (used - fixed)) % max(1, amount - fixed)
        return jnp.zeros((amount,), jnp.int32).at[order[jnp.where(places < fixed, places, passed)]].set(jnp.asarray(tallies, jnp.int32))

    tallies = jnp.where(number % 4 == 0, named(packed, number // 4), named(usual, number - number // 4 - 1))
    mixed = jax.random.permutation(jax.random.fold_in(own, 3), amount)
    donor, sink = mixed[0:amount // 2 * 2:2], mixed[1:amount // 2 * 2:2]
    room = jnp.minimum(tallies[donor] - 1, reach - tallies[sink]) // 2
    room = jnp.where((donor == order[0]) | (sink == order[0]) | (tallies[sink] == 0), 0, jnp.maximum(room, 0))
    passed = jax.random.randint(jax.random.fold_in(own, 4), (amount // 2,), 0, 1 << 20) % (room + 1)
    tallies = tallies.at[donor].add(-passed).at[sink].add(passed)
    items = jnp.searchsorted(jnp.cumsum(tallies), jnp.arange(rows * top), side="right").astype(jnp.int32)
    table = items.reshape(top, rows).T
    table = table[jax.random.permutation(jax.random.fold_in(own, 1), rows)]
    offset_by = jax.random.randint(jax.random.fold_in(own, 2), (rows, 1), 0, top)
    return jnp.take_along_axis(table, (jnp.arange(top)[None, :] + offset_by) % top, axis=1)


def portions_of(number_of, total, limit, lean, full):
    loads = [(1 << 20) // math.isqrt(grade ** lean) + 1 for grade in range(1, number_of + 1)]
    largest = limit if full else min(limit, max(-(-total // number_of), total * loads[0] // sum(loads)))
    least = 1 if total - largest >= number_of - 1 else 0
    given, spare = [largest] + [least] * (number_of - 1), total - largest - least * (number_of - 1)
    while spare > 0:
        candidates = [i for i in range(1, number_of) if given[i] < largest] or [i for i in range(1, number_of) if given[i] < limit]
        pool, left = sum([loads[i] for i in candidates]), spare
        for i in candidates:
            addition = min(limit - given[i], max(1, left * loads[i] // pool), spare)
            given[i] = given[i] + addition
            spare = spare - addition
    return np.array(given)


def scatter_about(own_key, extent, width, bound, shards=(), kind=jnp.bfloat16):
    entries = jax.random.normal(own_key, extent, jnp.float32) * width
    if len(shards) > 0:
        entries = shard_levels(own_key, extent, shards, -0.22, 0.18) * entries
    return jnp.clip(entries, min=-bound, max=bound).astype(kind)


def setup_inputs(seed: int = 0) -> dict:
    seeds = jax.random.split(jax.random.key(seed), 9)
    hidden = scatter_about(seeds[0], (SPANS, SPAN, D), 1.0, 6.0, ((0, 16), (1, 8), (2, 2)))
    kv_weight = scatter_about(seeds[1], (D, 2, KVH * HD), D ** -0.5, 0.09375, ((0, 16), (2, 2)))
    queries = draw_queries(jax.random.fold_in(seeds[8], 71), 0)
    kv_pool = scatter_about(seeds[3], (POOL, PAGE, 2, KVH * HD), 1.0, 6.0, ((0, 16), (3, 2)))
    hit_host_keys = jax.random.split(jax.random.fold_in(seeds[4], 1), SPANS * HITS // HITS)
    hit_host_turns = jax.random.permutation(jax.random.fold_in(seeds[4], 3), SPANS * HITS // HITS)
    hit_host = jax.vmap(lambda own, number: shared_out(jax.random.fold_in(seeds[4], 2), own, number, HITS, N_CACHE, 1, CAP, 2))(hit_host_keys, hit_host_turns).reshape((SPANS, HITS, 1))
    hit_page = place_ends(ranked(seeds[5], (SPANS, HITS), PAGES_DEV, 2), jax.random.fold_in(seeds[5], 3), 0, PAGES_DEV - 1).astype(jnp.int32)
    hit_request = place_ends(jax.random.randint(seeds[6], (SPANS, HITS), 0, REQS), jax.random.fold_in(seeds[6], 1), 0, REQS - 1).astype(jnp.int32)
    segment_ids = jax.vmap(lambda own: jnp.searchsorted(jnp.cumsum(ragged(own, REQS, SPAN, SPAN // 2, 2)), jnp.arange(SPAN), side="right"))(jax.random.split(seeds[7], SPANS)).reshape((SPANS, SPAN)).astype(jnp.int32)
    return dict(hidden=hidden, kv_weight=kv_weight, queries=queries, kv_pool=kv_pool, hit_host=hit_host, hit_page=hit_page, hit_request=hit_request, segment_ids=segment_ids)


masked_score = -1e+30

def reference(hidden, kv_weight, queries, kv_pool, hit_host, hit_page, hit_request, segment_ids):
    flat_weight = kv_weight.reshape(D, 2 * KVH * HD)

    def project(span_rows):
        mixed = jnp.dot(span_rows, flat_weight, preferred_element_type=jnp.float32)
        return mixed.astype(jnp.bfloat16).reshape(SPAN, 2, KVH * HD)
    kv_new = lax.map(project, hidden)
    owners = hit_host[:, :, 0]
    page_rows = (owners * PAGES_DEV + hit_page).astype(jnp.int32)
    prefix = kv_pool[page_rows]
    group_size = QH // KVH
    scale = 1.0 / math.sqrt(HD)
    key_count = HITS * PAGE + SPAN

    def one_span(operands):
        span_queries, span_kv, span_prefix, span_requests, span_segments = operands
        all_keys = jnp.concatenate([span_prefix.reshape(HITS * PAGE, 2, KVH * HD), span_kv], axis=0)
        key_segments = jnp.concatenate([jnp.repeat(span_requests, PAGE), span_segments]).astype(jnp.int32)
        positions = jnp.arange(SPAN, dtype=jnp.int32)
        key_positions = jnp.concatenate([jnp.full((HITS * PAGE,), -1, jnp.int32), positions])
        allowed = (key_segments[None, :] == span_segments[:, None]) & (key_positions[None, :] <= positions[:, None])
        key_heads = all_keys.reshape(key_count, 2, KVH, HD).transpose(2, 0, 1, 3)
        query_heads = span_queries.reshape(LAYERS, SPAN, KVH, group_size, HD).transpose(2, 0, 1, 3, 4)

        def one_group(pair):
            group_queries, group_keys = pair
            scores = jnp.einsum('ltqe,ne->ltqn', group_queries.astype(jnp.float32), group_keys[:, 0].astype(jnp.float32)) * scale
            scores = jnp.where(allowed[None, :, None, :], scores, masked_score)
            peak = lax.optimization_barrier(jnp.max(scores, axis=-1, keepdims=True))
            probs = jnp.where(allowed[None, :, None, :], jnp.exp(scores - peak), 0.0)
            total = lax.optimization_barrier(jnp.sum(probs, axis=-1, keepdims=True))
            probs_low = lax.optimization_barrier(probs.astype(jnp.bfloat16))
            summed = jnp.einsum('ltqn,ne->ltqe', probs_low.astype(jnp.float32), group_keys[:, 1].astype(jnp.float32))
            return summed / total
        grouped = lax.map(one_group, (query_heads, key_heads))
        return grouped.transpose(1, 2, 0, 3, 4).reshape(LAYERS, SPAN, QH * HD).astype(jnp.bfloat16)
    attended = lax.map(one_span, (queries.transpose(1, 0, 2, 3), kv_new, prefix, hit_request, segment_ids))
    return (attended.transpose(1, 0, 2, 3), kv_new)
```

```python
import math

import jax
import jax.numpy as jnp
from jax import lax
from jax.experimental import pallas as pl
from jax.experimental.pallas import tpu as pltpu
from jax.sharding import PartitionSpec as P

HD = 128
CAP = 2
HEADS = 4
GROUP = 4
TOK = 128
LAYERS = 2
HITS = 11
ROWS = LAYERS * GROUP * TOK
MASKED = -1e30
VMEM_LIMIT = 56 * 1024 * 1024

CACHE_UP = [(i, (i + 2) % 16) for i in range(16)]
CACHE_DOWN = [(i, (i - 2) % 16) for i in range(16)]
CACHE_NEAR = [(i, i ^ 1) for i in range(16)]
CORE = [(i, i ^ 1) for i in range(8)]
XPAIR = [(i, i ^ 2) for i in range(8)]
XUP = [(i, (i + 2) % 8) for i in range(8)]
XDOWN = [(i, (i - 2) % 8) for i in range(8)]
XFAR = [(i, (i + 4) % 8) for i in range(8)]
HEAD = [(0, 1), (1, 0)]
ANY = pl.BlockSpec(memory_space=pl.ANY)
SMEM = pl.BlockSpec(memory_space=pltpu.SMEM)
VMEM = pl.BlockSpec(memory_space=pltpu.VMEM)


def pack_kernel(choice, pool, out):
    for i in range(out.shape[0]):
        out[i] = pool[choice[i]]


def take_rows(choice, pool, count):
    return pl.pallas_call(
        pack_kernel,
        out_shape=jax.ShapeDtypeStruct((count,) + pool.shape[1:], pool.dtype),
        in_specs=[SMEM, VMEM],
        out_specs=VMEM,
        compiler_params=pltpu.CompilerParams(vmem_limit_bytes=VMEM_LIMIT),
        cost_estimate=pl.CostEstimate(
            flops=0, bytes_accessed=2 * count * pool.shape[1] * pool.shape[2] * 2, transcendentals=0
        ),
    )(choice, pool)


def project_kernel(where, *refs):
    hidden = refs[:8]
    weights = refs[8:17]
    out, hid, wts, sems = refs[17:]
    head, core_x, z = where[0], where[1], where[2]
    copies = []

    def start(src, dst):
        copy = pltpu.make_async_copy(src, dst, sems.at[len(copies)])
        copy.start()
        copies.append(copy)

    for i in range(8):
        half, rel = i // 4, i % 4
        tokens = jnp.bitwise_xor(core_x, rel) * TOK
        columns = jnp.bitwise_xor(head, half) * 2048
        start(
            hidden[i],
            hid.at[pl.ds(pl.multiple_of(tokens, TOK), TOK), pl.ds(pl.multiple_of(columns, 2048), 2048)],
        )
    for i, shift in enumerate((0, -1, 1, -2, 2, -3, 3)):
        row = lax.rem(z + shift + 8, 8) * 512
        start(weights[i], wts.at[pl.ds(pl.multiple_of(row, 512), 512)])
    far = lax.rem(z + 4, 8) * 512
    start(weights[7], wts.at[pl.ds(pl.multiple_of(far, 512), 256)])
    start(weights[8], wts.at[pl.ds(pl.multiple_of(far + 256, 256), 256)])
    for copy in copies:
        copy.wait()
    out[...] = jnp.dot(hid[...], wts[...], preferred_element_type=jnp.float32).astype(out.dtype)


def project(where, hidden, weights):
    return pl.pallas_call(
        project_kernel,
        out_shape=jax.ShapeDtypeStruct((4 * TOK, 2 * HD), jnp.bfloat16),
        in_specs=[SMEM] + [ANY] * 17,
        out_specs=VMEM,
        scratch_shapes=[
            pltpu.VMEM((4 * TOK, 4096), jnp.bfloat16),
            pltpu.VMEM((4096, 2 * HD), jnp.bfloat16),
            pltpu.SemaphoreType.DMA((17,)),
        ],
        compiler_params=pltpu.CompilerParams(vmem_limit_bytes=VMEM_LIMIT),
        cost_estimate=pl.CostEstimate(
            flops=2 * 512 * 4096 * 256, bytes_accessed=6 * 1024 * 1024, transcendentals=0
        ),
    )(where, *hidden, *weights)


def attend_kernel(info, requests, queries, query_seg, key_seg, *refs):
    new_parts, page_parts = refs[:8], refs[8:16]
    out, own = refs[16:18]
    new, pages, scores, peak, total, weighted, chosen, sems = refs[18:]
    seq, first_block, low_seg, high_seg = info[0], info[1], info[2], info[3]
    copies = []
    for kind, (parts, dst) in enumerate(((page_parts, pages), (new_parts, new))):
        for i in range(8):
            x_shift, core_flip = i // 2, i % 2
            place = lax.rem(seq // 2 + x_shift, 4) * 2 + jnp.bitwise_xor(lax.rem(seq, 2), core_flip)
            copy = pltpu.make_async_copy(parts[i], dst.at[place], sems.at[kind * 8 + i])
            copy.start()
            copies.append(copy)
    count = jnp.int32(0)
    for slot in range(HITS):
        chosen[count] = jnp.int32(slot)
        wanted = (requests[slot] >= low_seg) & (requests[slot] <= high_seg)
        count = count + wanted.astype(jnp.int32)
    for copy in copies:
        copy.wait()
    seg = query_seg[...]
    seg_wide = jnp.broadcast_to(seg, (TOK, TOK))
    key_lane = lax.broadcasted_iota(jnp.int32, (TOK, TOK), 1)
    query_row = lax.broadcasted_iota(jnp.int32, (TOK, TOK), 0) + seq * TOK
    spans = seq - first_block + 1
    factor = math.log2(math.e) / math.sqrt(HD)

    pair = seq // 4
    part_rows = pl.ds(pl.multiple_of(lax.rem(seq, 4) * TOK, TOK), TOK)
    for g in range(HEADS):
        for j in range(2):
            own[:, (j * HEADS + g) * HD : (j * HEADS + g + 1) * HD] = new[
                pair * 4 + g, part_rows, j * HD : (j + 1) * HD
            ]

    def new_rows(g, block, j):
        start = pl.multiple_of(lax.rem(block, 4) * TOK, TOK)
        return new[(block // 4) * 4 + g, pl.ds(start, TOK), j * HD : (j + 1) * HD]

    def page_rows(g, slot, j):
        start = pl.multiple_of(slot * 64, 64)
        return jnp.concatenate(
            [pages[half * 4 + g, pl.ds(start, 64), j * HD : (j + 1) * HD] for half in range(2)], axis=0
        )

    for g in range(HEADS):
        rows = jnp.concatenate(
            [
                queries[layer, :, (g * GROUP + n) * HD : (g * GROUP + n + 1) * HD]
                for layer in range(LAYERS)
                for n in range(GROUP)
            ],
            axis=0,
        )

        def score(place, keys, bias):
            found = lax.dot_general(rows, keys, (((1,), (1,)), ((), ())), preferred_element_type=jnp.float32)
            found = (found.reshape(LAYERS * GROUP, TOK, TOK) + bias[None]).reshape(ROWS, TOK)
            scores[place] = found
            peak[...] = jnp.maximum(peak[...], found)

        peak[...] = jnp.full(peak.shape, MASKED, jnp.float32)

        def score_new(i, _):
            block = first_block + i
            allowed = (key_seg[block] == seg_wide) & (block * TOK + key_lane <= query_row)
            score(i, new_rows(g, block, 0), jnp.where(allowed, 0.0, MASKED))
            return 0

        def score_page(i, _):
            slot = chosen[i]
            allowed = seg_wide == requests[slot]
            score(spans + i, page_rows(g, slot, 0), jnp.where(allowed, 0.0, MASKED))
            return 0

        lax.fori_loop(0, spans, score_new, 0)
        lax.fori_loop(0, count, score_page, 0)
        peak[...] = jnp.broadcast_to(jnp.max(peak[...], axis=1, keepdims=True) * factor, peak.shape)
        total[...] = jnp.zeros(total.shape, jnp.float32)
        weighted[...] = jnp.zeros(weighted.shape, jnp.float32)

        def weigh(place, values):
            probs = jnp.exp2(scores[place] * factor - peak[...])
            total[...] += probs
            weighted[...] += jnp.dot(probs.astype(jnp.bfloat16), values, preferred_element_type=jnp.float32)

        def weigh_new(i, _):
            weigh(i, new_rows(g, first_block + i, 1))
            return 0

        def weigh_page(i, _):
            weigh(spans + i, page_rows(g, chosen[i], 1))
            return 0

        lax.fori_loop(0, spans, weigh_new, 0)
        lax.fori_loop(0, count, weigh_page, 0)
        result = (weighted[...] / jnp.sum(total[...], axis=1, keepdims=True)).astype(jnp.bfloat16)
        for layer in range(LAYERS):
            for n in range(GROUP):
                i = layer * GROUP + n
                out[layer, :, (g * GROUP + n) * HD : (g * GROUP + n + 1) * HD] = result[i * TOK : (i + 1) * TOK]


def attend(info, requests, queries, query_seg, key_seg, new_parts, page_parts):
    return pl.pallas_call(
        attend_kernel,
        out_shape=(
            jax.ShapeDtypeStruct(queries.shape, jnp.bfloat16),
            jax.ShapeDtypeStruct((TOK, 2 * HEADS * HD), jnp.bfloat16),
        ),
        in_specs=[SMEM, SMEM, VMEM, VMEM, VMEM] + [ANY] * 16,
        out_specs=(VMEM, VMEM),
        scratch_shapes=[
            pltpu.VMEM((8, 4 * TOK, 2 * HD), jnp.bfloat16),
            pltpu.VMEM((8, HITS * 64, 2 * HD), jnp.bfloat16),
            pltpu.VMEM((HITS + 8, ROWS, TOK), jnp.float32),
            pltpu.VMEM((ROWS, TOK), jnp.float32),
            pltpu.VMEM((ROWS, TOK), jnp.float32),
            pltpu.VMEM((ROWS, HD), jnp.float32),
            pltpu.SMEM((HITS + 1,), jnp.int32),
            pltpu.SemaphoreType.DMA((16,)),
        ],
        compiler_params=pltpu.CompilerParams(vmem_limit_bytes=VMEM_LIMIT),
        cost_estimate=pl.CostEstimate(
            flops=5 * 10**9, bytes_accessed=8 * 1024 * 1024, transcendentals=10**7
        ),
    )(info, requests, queries, query_seg, key_seg, *new_parts, *page_parts)


def seq_gather(block):
    across = [
        block,
        lax.ppermute(block, "seq", XDOWN),
        lax.ppermute(block, "seq", XFAR),
        lax.ppermute(block, "seq", XUP),
    ]
    parts = []
    for piece in across:
        parts += [piece, lax.ppermute(piece, "seq", CORE)]
    return parts


def on_device(hidden, kv_weight, queries, kv_pool, hit_host, hit_page, hit_request, segment_ids):
    span = lax.axis_index("cache")
    seq = lax.axis_index("seq")
    head = lax.axis_index("head")
    quarter = lax.rem(seq, 4)

    own_cols = lax.dynamic_slice_in_dim(kv_weight, quarter * HD, HD, 2).reshape(256, 2 * HD)
    near_cols = lax.ppermute(own_cols, "cache", CACHE_NEAR)
    odd = lax.rem(span, 2) == 1
    both = jnp.concatenate(
        [jnp.where(odd, near_cols, own_cols), jnp.where(odd, own_cols, near_cols)], axis=0
    )
    ups, downs = [both], [both]
    for step in range(3):
        ups.append(lax.ppermute(ups[-1], "cache", CACHE_UP))
        downs.append(lax.ppermute(downs[-1], "cache", CACHE_DOWN))
    far_a = lax.ppermute(ups[3][:256], "cache", CACHE_UP)
    far_b = lax.ppermute(downs[3][256:], "cache", CACHE_DOWN)
    weights = [both, ups[1], downs[1], ups[2], downs[2], ups[3], downs[3], far_a, far_b]

    mine = hidden[0]
    other = lax.ppermute(mine, "head", HEAD)
    rows = []
    for half in (mine, other):
        across = lax.ppermute(half, "seq", XPAIR)
        rows += [half, lax.ppermute(half, "seq", CORE), across, lax.ppermute(across, "seq", CORE)]

    owners = hit_host[:, :, 0]
    slots = jnp.arange(HITS)
    same = (owners[:, :, None] == owners[:, None, :]) & (slots[:, None] < slots[None, :])[None]
    rank = jnp.sum(same, axis=1)
    picked = (owners == span)[:, None, :] & (rank[:, None, :] == jnp.arange(CAP)[None, :, None])
    choice = jnp.sum(jnp.where(picked, hit_page[:, None, :], 0), axis=2).reshape(-1).astype(jnp.int32)
    received = (
        lax.dynamic_index_in_dim(owners, span, 0, keepdims=False) * CAP
        + lax.dynamic_index_in_dim(rank, span, 0, keepdims=False)
    ).astype(jnp.int32)
    pool = lax.dynamic_slice(
        kv_pool, (0, (seq // 4) * 64, 0, quarter * HD), (kv_pool.shape[0], 64, 2, HD)
    ).reshape(kv_pool.shape[0], 64, 2 * HD)
    packed = take_rows(choice, pool, 16 * CAP)
    arrived = lax.all_to_all(packed, "cache", split_axis=0, concat_axis=0, tiled=True)
    prefix = take_rows(received, arrived, HITS).reshape(HITS * 64, 2 * HD)
    page_parts = seq_gather(prefix)

    block = project(jnp.stack([head, quarter, span // 2]).astype(jnp.int32), rows, weights)
    new_parts = seq_gather(block)

    segments = segment_ids[0]
    query_seg = lax.dynamic_slice_in_dim(segments, seq * TOK, TOK)
    low, high = query_seg[0], query_seg[TOK - 1]
    first = jnp.sum(segments < low) // TOK
    info = jnp.stack([seq, first, low, high]).astype(jnp.int32)
    requests = lax.dynamic_index_in_dim(hit_request, span, 0, keepdims=False)
    attended, own = attend(
        info,
        requests,
        queries[:, 0],
        query_seg.reshape(TOK, 1),
        segments.reshape(8, 1, TOK),
        new_parts,
        page_parts,
    )
    return attended[:, None], own.reshape(1, TOK, 2, HEADS * HD)


def solution(mesh):
    return jax.shard_map(
        on_device,
        mesh=mesh,
        in_specs=(
            P("cache", "seq", "head"),
            P("cache", None, "head"),
            P(None, "cache", "seq", "head"),
            P("cache", None, None, "head"),
            P(),
            P(),
            P(),
            P("cache", None),
        ),
        out_specs=(P(None, "cache", "seq", "head"), P("cache", "seq", None, "head")),
        check_vma=False,
    )
```

```python
import math

import jax
import jax.numpy as jnp
from jax import lax
from jax.experimental import pallas as pl
from jax.experimental.pallas import tpu as pltpu
from jax.sharding import PartitionSpec as P

HD = 128
CAP = 2
HEADS = 4
GROUP = 4
TOK = 128
LAYERS = 2
CHUNKS = LAYERS * GROUP
ROWS = CHUNKS * TOK
WIDTH = 1024
HITS = 11
HALF = 64
SPANS = 16
MASKED = -1e30
NEVER = 1e30
FACTOR = math.log2(math.e) / math.sqrt(HD)
VMEM_LIMIT = 16 * 1024 * 1024

CACHE_UP = [(i, (i + 2) % 16) for i in range(16)]
CACHE_DOWN = [(i, (i - 2) % 16) for i in range(16)]
CACHE_NEAR = [(i, i ^ 1) for i in range(16)]
CORE = [(i, i ^ 1) for i in range(8)]
XPAIR = [(i, i ^ 2) for i in range(8)]
XUP = [(i, (i + 2) % 8) for i in range(8)]
XDOWN = [(i, (i - 2) % 8) for i in range(8)]
XFAR = [(i, (i + 4) % 8) for i in range(8)]
HEAD = [(0, 1), (1, 0)]
ANY = pl.BlockSpec(memory_space=pl.ANY)
SMEM = pl.BlockSpec(memory_space=pltpu.SMEM)
VMEM = pl.BlockSpec(memory_space=pltpu.VMEM)


def params():
    return pltpu.CompilerParams(vmem_limit_bytes=VMEM_LIMIT)


def cost(flops, transferred, exps=0):
    return pl.CostEstimate(flops=flops, bytes_accessed=transferred, transcendentals=exps)


def bf16(*shape):
    return jax.ShapeDtypeStruct(shape, jnp.bfloat16)


def f32(*shape):
    return jax.ShapeDtypeStruct(shape, jnp.float32)


def pack_kernel(hosts, pages, pool, *refs):
    out = refs[-1]
    me = lax.axis_index("cache")

    def one_span(c, _):
        found, first, second = jnp.int32(0), jnp.int32(0), jnp.int32(0)
        for h in range(HITS):
            here = hosts[c, h] == me
            page = pages[c, h]
            first = jnp.where(here & (found == 0), page, first)
            second = jnp.where(here & (found == 1), page, second)
            found = found + here.astype(jnp.int32)
        out[c * CAP] = pool[first]
        out[c * CAP + 1] = pool[second]
        return 0

    lax.fori_loop(0, SPANS, one_span, 0)


def pack(hosts, pages, pool, *after):
    return pl.pallas_call(
        pack_kernel,
        name="pack",
        out_shape=bf16(SPANS * CAP, HALF, 2 * HD),
        in_specs=[SMEM, SMEM, VMEM] + [VMEM] * len(after),
        out_specs=VMEM,
        compiler_params=params(),
        cost_estimate=cost(0, 2 * 2**20),
    )(hosts, pages, pool, *after)


def unpack_kernel(hosts, arrived, after, out):
    me = lax.axis_index("cache")
    for h in range(HITS):
        host = hosts[me, h]
        place = host * CAP
        for other in range(h):
            place = place + (hosts[me, other] == host).astype(jnp.int32)
        out[h * HALF : (h + 1) * HALF] = arrived[place]


def unpack(hosts, arrived, after):
    return pl.pallas_call(
        unpack_kernel,
        name="unpack",
        out_shape=bf16(HITS * HALF, 2 * HD),
        in_specs=[SMEM, VMEM, VMEM],
        out_specs=VMEM,
        compiler_params=params(),
        cost_estimate=cost(0, 2**20),
    )(hosts, arrived, after)


def project_near_kernel(*refs):
    hidden, weights = refs[:8], refs[8:15]
    partial, far_hidden, hid, wts = refs[15:]
    head = lax.axis_index("head")
    quarter = lax.rem(lax.axis_index("seq"), 4)
    z = lax.axis_index("cache") // 2
    far = pl.multiple_of(lax.rem(z + 4, 8) * 512, 512)
    for i in range(8):
        half, rel = i // 4, i % 4
        tokens = pl.multiple_of(jnp.bitwise_xor(quarter, rel) * TOK, TOK)
        columns = pl.multiple_of(jnp.bitwise_xor(head, half) * 2048, 2048)
        hid[pl.ds(tokens, TOK), pl.ds(columns, 2048)] = hidden[i][...]
    for i, shift in enumerate((0, -1, 1, -2, 2, -3, 3)):
        row = pl.multiple_of(lax.rem(z + shift + 8, 8) * 512, 512)
        wts[pl.ds(row, 512)] = weights[i][...]
    wts[pl.ds(far, 512)] = jnp.zeros((512, 2 * HD), jnp.bfloat16)
    partial[...] = jnp.dot(hid[...], wts[...], preferred_element_type=jnp.float32)
    far_hidden[...] = hid[:, pl.ds(far, 512)]


def project_near(hidden, weights):
    return pl.pallas_call(
        project_near_kernel,
        name="project_near",
        out_shape=(f32(4 * TOK, 2 * HD), bf16(4 * TOK, 512)),
        in_specs=[VMEM] * 15,
        out_specs=(VMEM, VMEM),
        scratch_shapes=[
            pltpu.VMEM((4 * TOK, 4096), jnp.bfloat16),
            pltpu.VMEM((4096, 2 * HD), jnp.bfloat16),
        ],
        compiler_params=params(),
        cost_estimate=cost(2 * 512 * 3584 * 256, 6 * 2**20),
    )(*hidden, *weights)


def project_far_kernel(partial, far_hidden, weights, out):
    out[...] = (
        partial[...] + jnp.dot(far_hidden[...], weights[...], preferred_element_type=jnp.float32)
    ).astype(out.dtype)


def project_far(partial, far_hidden, weights):
    return pl.pallas_call(
        project_far_kernel,
        name="project_far",
        out_shape=bf16(4 * TOK, 2 * HD),
        in_specs=[VMEM] * 3,
        out_specs=VMEM,
        compiler_params=params(),
        cost_estimate=cost(2 * 512 * 512 * 256, 2**20),
    )(partial, far_hidden, weights)


def absorb(places, pieces, rows, limits, bias, state):
    peaks, totals, sums = state
    steps = [(g, part) for g in range(HEADS) for part in range(ROWS // WIDTH)]
    repeat = WIDTH // TOK
    wide = None if limits is None else [jnp.concatenate([limit] * repeat, axis=1) for limit in limits]
    if bias is not None:
        bias = jnp.concatenate([bias] * repeat, axis=1)
    flipped = [jnp.transpose(piece[:, HD:]) for piece in pieces]

    def raw(i):
        g, part = steps[i]
        place = places[g]
        return jnp.dot(
            pieces[g][:, :HD], rows[place, :, part * WIDTH : (part + 1) * WIDTH], preferred_element_type=jnp.float32
        )

    def soften(i, found):
        g, part = steps[i]
        place = places[g]
        where = slice(part * WIDTH, (part + 1) * WIDTH)
        scaled = found * FACTOR
        if bias is not None:
            scaled = scaled + bias
        halves = scaled.shape[0] // TOK
        largest = None
        for h in range(halves):
            block = jnp.max(scaled[h * TOK : (h + 1) * TOK].reshape(TOK // 8, 8, WIDTH), axis=0)
            if wide is not None:
                block = jnp.where(wide[h], block, MASKED)
            largest = block if largest is None else jnp.maximum(largest, block)
        before = peaks[place, 0:1, where]
        peak = jnp.maximum(before, jnp.max(largest, axis=0, keepdims=True))
        shrink = jnp.exp2(before - peak)
        probs = []
        for h in range(halves):
            level = peak if wide is None else jnp.where(wide[h], peak, NEVER)
            probs.append(jnp.exp2(scaled[h * TOK : (h + 1) * TOK] - level))
        total = totals[place, :, where] * shrink
        for block in probs:
            total = total + jnp.sum(block.reshape(TOK // 8, 8, WIDTH), axis=0)
        peaks[place, 0:1, where] = peak
        totals[place, :, where] = total
        return jnp.concatenate([block.astype(jnp.bfloat16) for block in probs], axis=0), shrink

    def add(i, probs, shrink):
        g, part = steps[i]
        place = places[g]
        where = slice(part * WIDTH, (part + 1) * WIDTH)
        sums[place, :, where] = sums[place, :, where] * shrink + jnp.dot(
            flipped[g], probs, preferred_element_type=jnp.float32
        )

    found, held = raw(0), None
    for i in range(len(steps)):
        following = raw(i + 1) if i + 1 < len(steps) else None
        if held is not None:
            add(i - 1, *held)
        held = soften(i, found)
        found = following
    add(len(steps) - 1, *held)


def relay_kernel(*refs):
    out = refs[-1]
    for i in range(4):
        out[i] = refs[i][...]


def relay(blocks, after):
    return pl.pallas_call(
        relay_kernel,
        name="relay",
        out_shape=bf16(4, *blocks[0].shape),
        in_specs=[VMEM] * 4 + [VMEM] * len(after),
        out_specs=VMEM,
        compiler_params=params(),
        cost_estimate=cost(0, 2**21),
    )(*blocks, *after)


def stage_kernel(hidden, own_cols, near_cols, queries, query_seg, key_seg, hosts, pool, sent, both, rows, bias):
    seq = lax.axis_index("seq")
    odd = lax.rem(lax.axis_index("cache"), 2)
    sent[...] = hidden[...]
    both[pl.ds(pl.multiple_of(odd * 256, 256), 256)] = own_cols[...]
    both[pl.ds(pl.multiple_of(256 - odd * 256, 256), 256)] = near_cols[...]
    for g in range(HEADS):
        for chunk in range(CHUNKS):
            column = (g * GROUP + chunk % GROUP) * HD
            rows[g, :, chunk * TOK : (chunk + 1) * TOK] = jnp.transpose(
                queries[chunk // GROUP, :, column : column + HD]
            )
    query_wide = jnp.broadcast_to(query_seg[...], (TOK, TOK))
    key_row = lax.broadcasted_iota(jnp.int32, (TOK, TOK), 0)
    query_lane = lax.broadcasted_iota(jnp.int32, (TOK, TOK), 1) + seq * TOK
    for block in range(8):
        key_wide = jnp.transpose(jnp.broadcast_to(key_seg[block : block + 1], (TOK, TOK)))
        allowed = (key_wide == query_wide) & (key_row + block * TOK <= query_lane)
        bias[block // 2, (block % 2) * TOK : (block % 2 + 1) * TOK] = jnp.where(allowed, 0.0, MASKED)


def stage(hidden, own_cols, near_cols, queries, query_seg, key_seg, hosts, pool):
    return pl.pallas_call(
        stage_kernel,
        name="stage",
        out_shape=(
            bf16(*hidden.shape),
            bf16(512, 2 * HD),
            bf16(HEADS, HD, ROWS),
            f32(4, 2 * TOK, TOK),
        ),
        in_specs=[VMEM] * 6 + [SMEM, VMEM],
        out_specs=(VMEM,) * 4,
        compiler_params=params(),
        cost_estimate=cost(0, 3 * 2**20),
    )(hidden, own_cols, near_cols, queries, query_seg, key_seg, hosts, pool)


def ring_place():
    seq = lax.axis_index("seq")
    x, core = seq // 2, lax.rem(seq, 2)
    places = [half * 2 + jnp.bitwise_xor(core, flip) for half in range(2) for flip in range(2)]
    return seq, x, places


def attend_new_kernel(segments, rows, bias, mine, theirs, after, own, peak, total, summed):
    seq, x, places = ring_place()
    refs = (mine, theirs)
    low = segments[seq * TOK]
    last = seq // 2
    first = jnp.int32(0)
    for k in range(4):
        first = first + (segments[k * 2 * TOK + 2 * TOK - 1] < low).astype(jnp.int32)
    part_rows = pl.ds(pl.multiple_of(lax.rem(seq, 4) * TOK, TOK), TOK)
    core = lax.rem(seq, 2)
    for g in range(HEADS):
        shift = lax.rem((x // 2) * 2 + g // 2 - x + 4, 4)
        flip = jnp.bitwise_xor(core, g % 2)
        block = jnp.where(flip == 0, mine[shift, part_rows, :], theirs[shift, part_rows, :])
        own[:, 0, g * HD : (g + 1) * HD] = block[:, :HD]
        own[:, 1, g * HD : (g + 1) * HD] = block[:, HD:]
    peak[...] = jnp.full(peak.shape, MASKED, jnp.float32)
    total[...] = jnp.zeros(total.shape, jnp.float32)
    summed[...] = jnp.zeros(summed.shape, jnp.float32)

    def one_pair(i, _):
        k = last - i
        where = pl.ds(pl.multiple_of(lax.rem(k, 2) * 2 * TOK, 2 * TOK), 2 * TOK)
        pieces = [
            refs[flip][lax.rem((k // 2) * 2 + half - x + 4, 4), where, :] for half in range(2) for flip in range(2)
        ]
        absorb(places, pieces, rows, None, bias[k], (peak, total, summed))
        return 0

    lax.fori_loop(0, last - first + 1, one_pair, 0)


def attend_new(segments, rows, bias, mine, theirs, after):
    return pl.pallas_call(
        attend_new_kernel,
        name="attend_new",
        out_shape=(
            bf16(TOK, 2, HEADS * HD),
            f32(HEADS, 8, ROWS),
            f32(HEADS, 8, ROWS),
            f32(HEADS, HD, ROWS),
        ),
        in_specs=[SMEM] + [VMEM] * 5,
        out_specs=(VMEM,) * 4,
        compiler_params=params(),
        cost_estimate=cost(2 * 10**9, 6 * 2**20, 3 * 10**6),
    )(segments, rows, bias, mine, theirs, after)


def attend_pages_kernel(
    requests, segments, query_seg, rows, peak_in, total_in, summed_in, mine, theirs, out, peak, total, summed, chosen
):
    seq, x, places = ring_place()
    span = lax.axis_index("cache")
    refs = (mine, theirs)
    low, high = segments[seq * TOK], segments[seq * TOK + TOK - 1]
    count = jnp.int32(0)
    for slot in range(HITS):
        chosen[count] = jnp.int32(slot)
        request = requests[span, slot]
        count = count + ((request >= low) & (request <= high)).astype(jnp.int32)
    peak[...] = peak_in[...]
    total[...] = total_in[...]
    summed[...] = summed_in[...]
    seg = query_seg[...]

    def one_pair(pair, _):
        slots = [chosen[2 * pair], chosen[jnp.minimum(2 * pair + 1, count - 1)]]
        second = jnp.where(2 * pair + 1 < count, requests[span, slots[1]], -1)
        limits = [seg == requests[span, slots[0]], seg == second]
        pieces = [
            jnp.concatenate(
                [
                    refs[flip][
                        lax.rem(2 * part + half - x + 4, 4), pl.ds(pl.multiple_of(slot * HALF, HALF), HALF), :
                    ]
                    for slot in slots
                    for part in range(2)
                ],
                axis=0,
            )
            for half in range(2)
            for flip in range(2)
        ]
        absorb(places, pieces, rows, limits, None, (peak, total, summed))
        return 0

    lax.fori_loop(0, (count + 1) // 2, one_pair, 0)
    for g in range(HEADS):
        for chunk in range(CHUNKS):
            where = slice(chunk * TOK, (chunk + 1) * TOK)
            value = summed[g, :, where] / jnp.sum(total[g, :, where], axis=0, keepdims=True)
            column = (g * GROUP + chunk % GROUP) * HD
            out[chunk // GROUP, :, column : column + HD] = jnp.transpose(value.astype(jnp.bfloat16))


def attend_pages(requests, segments, query_seg, rows, state, mine, theirs):
    return pl.pallas_call(
        attend_pages_kernel,
        name="attend_pages",
        out_shape=bf16(LAYERS, TOK, HEADS * GROUP * HD),
        in_specs=[SMEM, SMEM] + [VMEM] * 7,
        out_specs=VMEM,
        scratch_shapes=[
            pltpu.VMEM((HEADS, 8, ROWS), jnp.float32),
            pltpu.VMEM((HEADS, 8, ROWS), jnp.float32),
            pltpu.VMEM((HEADS, HD, ROWS), jnp.float32),
            pltpu.SMEM((HITS + 1,), jnp.int32),
        ],
        compiler_params=params(),
        cost_estimate=cost(3 * 10**9, 6 * 2**20, 5 * 10**6),
    )(requests, segments, query_seg, rows, *state, mine, theirs)


def seq_gather(block, *after):
    mine = relay(
        [
            block,
            lax.ppermute(block, "seq", XDOWN),
            lax.ppermute(block, "seq", XFAR),
            lax.ppermute(block, "seq", XUP),
        ],
        after,
    )
    return mine, lax.ppermute(mine, "seq", CORE)


def on_device(hidden, kv_weight, queries, kv_pool, hit_host, hit_page, hit_request, segment_ids):
    seq = lax.axis_index("seq")
    quarter = lax.rem(seq, 4)
    segments = segment_ids[0]
    query_seg = lax.dynamic_slice_in_dim(segments, seq * TOK, TOK).reshape(1, TOK)

    own_cols = lax.dynamic_slice_in_dim(kv_weight, quarter * HD, HD, 2).reshape(256, 2 * HD)
    near_cols = lax.ppermute(own_cols, "cache", CACHE_NEAR)
    hosts = hit_host[:, :, 0]
    pool = lax.dynamic_slice(
        kv_pool, (0, (seq // 4) * HALF, 0, quarter * HD), (kv_pool.shape[0], HALF, 2, HD)
    ).reshape(kv_pool.shape[0], HALF, 2 * HD)
    mine, both, rows, bias = stage(
        hidden[0], own_cols, near_cols, queries[:, 0], query_seg, segments.reshape(8, TOK), hosts, pool
    )
    ups, downs = [both], [both]
    for step in range(3):
        ups.append(lax.ppermute(ups[-1], "cache", CACHE_UP))
        downs.append(lax.ppermute(downs[-1], "cache", CACHE_DOWN))
    far = lax.ppermute(ups[3], "cache", CACHE_UP)
    weights = [both, ups[1], downs[1], ups[2], downs[2], ups[3], downs[3]]

    other = lax.ppermute(mine, "head", HEAD)
    hidden_rows = []
    for half in (mine, other):
        across = lax.ppermute(half, "seq", XPAIR)
        hidden_rows += [half, lax.ppermute(half, "seq", CORE), across, lax.ppermute(across, "seq", CORE)]


    partial, far_hidden = project_near(hidden_rows, weights)
    block = project_far(partial, far_hidden, far)
    packed = pack(hosts, hit_page, pool, block)
    arrived = lax.all_to_all(packed, "cache", split_axis=0, concat_axis=0, tiled=True)
    new_mine, new_theirs = seq_gather(block)
    prefix = unpack(hosts, arrived, new_theirs)
    own, *state = attend_new(segments, rows, bias, new_mine, new_theirs, prefix)
    page_mine, page_theirs = seq_gather(prefix, state[0])
    attended = attend_pages(hit_request, segments, query_seg, rows, state, page_mine, page_theirs)
    return attended[:, None], own[None]


def solution(mesh):
    return jax.shard_map(
        on_device,
        mesh=mesh,
        in_specs=(
            P("cache", "seq", "head"),
            P("cache", None, "head"),
            P(None, "cache", "seq", "head"),
            P("cache", None, None, "head"),
            P(),
            P(),
            P(),
            P("cache", None),
        ),
        out_specs=(P(None, "cache", "seq", "head"), P("cache", "seq", None, "head")),
        check_vma=False,
    )
```

```python
import math

import jax
import jax.numpy as jnp
from jax import lax
from jax.experimental import pallas as pl
from jax.experimental.pallas import tpu as pltpu
from jax.sharding import PartitionSpec as P

HD = 128
CAP = 2
HEADS = 4
GROUP = 4
TOK = 128
LAYERS = 2
CHUNKS = LAYERS * GROUP
ROWS = CHUNKS * TOK
WIDTH = 1024
HITS = 11
HALF = 64
SPANS = 16
MASKED = -1e30
NEVER = 1e30
FACTOR = math.log2(math.e) / math.sqrt(HD)
VMEM_LIMIT = 16 * 1024 * 1024

CACHE_UP = [(i, (i + 2) % 16) for i in range(16)]
CACHE_DOWN = [(i, (i - 2) % 16) for i in range(16)]
CACHE_NEAR = [(i, i ^ 1) for i in range(16)]
CORE = [(i, i ^ 1) for i in range(8)]
XPAIR = [(i, i ^ 2) for i in range(8)]
XUP = [(i, (i + 2) % 8) for i in range(8)]
XDOWN = [(i, (i - 2) % 8) for i in range(8)]
XFAR = [(i, (i + 4) % 8) for i in range(8)]
HEAD = [(0, 1), (1, 0)]
DIAGONAL = [(i, i ^ 5) for i in range(16)]
ANY = pl.BlockSpec(memory_space=pl.ANY)
SMEM = pl.BlockSpec(memory_space=pltpu.SMEM)
VMEM = pl.BlockSpec(memory_space=pltpu.VMEM)


def params():
    return pltpu.CompilerParams(vmem_limit_bytes=VMEM_LIMIT)


def cost(flops, transferred, exps=0):
    return pl.CostEstimate(flops=flops, bytes_accessed=transferred, transcendentals=exps)


def bf16(*shape):
    return jax.ShapeDtypeStruct(shape, jnp.bfloat16)


def f32(*shape):
    return jax.ShapeDtypeStruct(shape, jnp.float32)


def pack_kernel(hosts, pages, pool, *refs):
    out = refs[-1]
    me = lax.axis_index("cache")

    def one_span(c, _):
        found, first, second = jnp.int32(0), jnp.int32(0), jnp.int32(0)
        for h in range(HITS):
            here = hosts[c, h] == me
            page = pages[c, h]
            first = jnp.where(here & (found == 0), page, first)
            second = jnp.where(here & (found == 1), page, second)
            found = found + here.astype(jnp.int32)
        out[c * CAP] = pool[first]
        out[c * CAP + 1] = pool[second]
        return 0

    lax.fori_loop(0, SPANS, one_span, 0)


def pack(hosts, pages, pool, *after):
    return pl.pallas_call(
        pack_kernel,
        name="pack",
        out_shape=bf16(SPANS * CAP, HALF, 2 * HD),
        in_specs=[SMEM, SMEM, VMEM] + [VMEM] * len(after),
        out_specs=VMEM,
        compiler_params=params(),
        cost_estimate=cost(0, 2 * 2**20),
    )(hosts, pages, pool, *after)


def unpack_kernel(hosts, arrived, after, out):
    me = lax.axis_index("cache")
    for h in range(HITS):
        host = hosts[me, h]
        place = host * CAP
        for other in range(h):
            place = place + (hosts[me, other] == host).astype(jnp.int32)
        out[h * HALF : (h + 1) * HALF] = arrived[place]


def unpack(hosts, arrived, after):
    return pl.pallas_call(
        unpack_kernel,
        name="unpack",
        out_shape=bf16(HITS * HALF, 2 * HD),
        in_specs=[SMEM, VMEM, ANY],
        out_specs=VMEM,
        compiler_params=params(),
        cost_estimate=cost(0, 2**20),
    )(hosts, arrived, after)


def project_near_kernel(mine, theirs, *refs):
    weights = refs[:7]
    partial, far_hidden, hid, wts = refs[-4:]
    head = lax.axis_index("head")
    quarter = lax.rem(lax.axis_index("seq"), 4)
    z = lax.axis_index("cache") // 2
    far = pl.multiple_of(lax.rem(z + 4, 8) * 512, 512)
    for i in range(4):
        columns = pl.multiple_of(jnp.bitwise_xor(head, i // 2) * 2048, 2048)
        for flip, block in enumerate((mine, theirs)):
            tokens = pl.multiple_of(jnp.bitwise_xor(quarter, 2 * (i % 2) + flip) * TOK, TOK)
            hid[pl.ds(tokens, TOK), pl.ds(columns, 2048)] = block[i]
    for i, shift in enumerate((0, -1, 1, -2, 2, -3, 3)):
        row = pl.multiple_of(lax.rem(z + shift + 8, 8) * 512, 512)
        wts[pl.ds(row, 512)] = weights[i][...]
    wts[pl.ds(far, 512)] = jnp.zeros((512, 2 * HD), jnp.bfloat16)
    partial[...] = jnp.dot(hid[...], wts[...], preferred_element_type=jnp.float32)
    far_hidden[...] = hid[:, pl.ds(far, 512)]


def project_near(mine, theirs, weights):
    return pl.pallas_call(
        project_near_kernel,
        name="project_near",
        out_shape=(f32(4 * TOK, 2 * HD), bf16(4 * TOK, 512)),
        in_specs=[VMEM] * 9,
        out_specs=(VMEM, VMEM),
        scratch_shapes=[
            pltpu.VMEM((4 * TOK, 4096), jnp.bfloat16),
            pltpu.VMEM((4096, 2 * HD), jnp.bfloat16),
        ],
        compiler_params=params(),
        cost_estimate=cost(2 * 512 * 3584 * 256, 6 * 2**20),
    )(mine, theirs, *weights)


def project_far_kernel(partial, far_hidden, weights, out):
    out[...] = (
        partial[...] + jnp.dot(far_hidden[...], weights[...], preferred_element_type=jnp.float32)
    ).astype(out.dtype)


def project_far(partial, far_hidden, weights):
    return pl.pallas_call(
        project_far_kernel,
        name="project_far",
        out_shape=bf16(4 * TOK, 2 * HD),
        in_specs=[VMEM] * 3,
        out_specs=VMEM,
        compiler_params=params(),
        cost_estimate=cost(2 * 512 * 512 * 256, 2**20),
    )(partial, far_hidden, weights)


def absorb(places, pieces, rows, limits, bias, state):
    peaks, totals, sums = state
    steps = [(g, part) for g in range(HEADS) for part in range(ROWS // WIDTH)]
    repeat = WIDTH // TOK
    wide = None if limits is None else [jnp.concatenate([limit] * repeat, axis=1) for limit in limits]
    if bias is not None:
        bias = jnp.concatenate([bias] * repeat, axis=1)
    flipped = [jnp.transpose(piece[:, HD:]) for piece in pieces]

    def raw(i):
        g, part = steps[i]
        place = places[g]
        return jnp.dot(
            pieces[g][:, :HD], rows[place, :, part * WIDTH : (part + 1) * WIDTH], preferred_element_type=jnp.float32
        )

    def soften(i, found):
        g, part = steps[i]
        place = places[g]
        where = slice(part * WIDTH, (part + 1) * WIDTH)
        scaled = found * FACTOR
        if bias is not None:
            scaled = scaled + bias
        halves = scaled.shape[0] // TOK
        largest = None
        for h in range(halves):
            block = jnp.max(scaled[h * TOK : (h + 1) * TOK].reshape(TOK // 8, 8, WIDTH), axis=0)
            if wide is not None:
                block = jnp.where(wide[h], block, MASKED)
            largest = block if largest is None else jnp.maximum(largest, block)
        before = peaks[place, 0:1, where]
        peak = jnp.maximum(before, jnp.max(largest, axis=0, keepdims=True))
        shrink = jnp.exp2(before - peak)
        probs = []
        for h in range(halves):
            level = peak if wide is None else jnp.where(wide[h], peak, NEVER)
            probs.append(jnp.exp2(scaled[h * TOK : (h + 1) * TOK] - level))
        total = totals[place, :, where] * shrink
        for block in probs:
            total = total + jnp.sum(block.reshape(TOK // 8, 8, WIDTH), axis=0)
        peaks[place, 0:1, where] = peak
        totals[place, :, where] = total
        return jnp.concatenate([block.astype(jnp.bfloat16) for block in probs], axis=0), shrink

    def add(i, probs, shrink):
        g, part = steps[i]
        place = places[g]
        where = slice(part * WIDTH, (part + 1) * WIDTH)
        sums[place, :, where] = sums[place, :, where] * shrink + jnp.dot(
            flipped[g], probs, preferred_element_type=jnp.float32
        )

    found, held = raw(0), None
    for i in range(len(steps)):
        following = raw(i + 1) if i + 1 < len(steps) else None
        if held is not None:
            add(i - 1, *held)
        held = soften(i, found)
        found = following
    add(len(steps) - 1, *held)


def relay_kernel(*refs):
    out = refs[-1]
    for i in range(4):
        out[i] = refs[i][...]


def relay(blocks, after):
    return pl.pallas_call(
        relay_kernel,
        name="relay",
        out_shape=bf16(4, *blocks[0].shape),
        in_specs=[VMEM] * 4 + [VMEM] * len(after),
        out_specs=VMEM,
        compiler_params=params(),
        cost_estimate=cost(0, 2**21),
    )(*blocks, *after)


def stage_kernel(hidden, pool, sent):
    sent[...] = hidden[...]


def stage(hidden, pool):
    return pl.pallas_call(
        stage_kernel,
        name="stage",
        out_shape=bf16(*hidden.shape),
        in_specs=[VMEM, VMEM],
        out_specs=VMEM,
        compiler_params=params(),
        cost_estimate=cost(0, 2**20),
    )(hidden, pool)


def order_kernel(own_cols, near_cols, hosts, pool, both):
    odd = lax.rem(lax.axis_index("cache"), 2)
    both[pl.ds(pl.multiple_of(odd * 256, 256), 256)] = own_cols[...]
    both[pl.ds(pl.multiple_of(256 - odd * 256, 256), 256)] = near_cols[...]


def order(own_cols, near_cols, hosts, pool):
    return pl.pallas_call(
        order_kernel,
        name="order",
        out_shape=bf16(512, 2 * HD),
        in_specs=[VMEM, VMEM, SMEM, VMEM],
        out_specs=VMEM,
        compiler_params=params(),
        cost_estimate=cost(0, 2**19),
    )(own_cols, near_cols, hosts, pool)


def prepare_kernel(queries, query_seg, key_seg, after, rows, bias):
    seq = lax.axis_index("seq")
    for g in range(HEADS):
        for chunk in range(CHUNKS):
            column = (g * GROUP + chunk % GROUP) * HD
            rows[g, :, chunk * TOK : (chunk + 1) * TOK] = jnp.transpose(
                queries[chunk // GROUP, :, column : column + HD]
            )
    query_wide = jnp.broadcast_to(query_seg[...], (TOK, TOK))
    key_row = lax.broadcasted_iota(jnp.int32, (TOK, TOK), 0)
    query_lane = lax.broadcasted_iota(jnp.int32, (TOK, TOK), 1) + seq * TOK
    for block in range(8):
        key_wide = jnp.transpose(jnp.broadcast_to(key_seg[block : block + 1], (TOK, TOK)))
        allowed = (key_wide == query_wide) & (key_row + block * TOK <= query_lane)
        bias[block // 2, (block % 2) * TOK : (block % 2 + 1) * TOK] = jnp.where(allowed, 0.0, MASKED)


def prepare(queries, query_seg, key_seg, after):
    return pl.pallas_call(
        prepare_kernel,
        name="prepare",
        out_shape=(bf16(HEADS, HD, ROWS), f32(4, 2 * TOK, TOK)),
        in_specs=[VMEM] * 4,
        out_specs=(VMEM,) * 2,
        compiler_params=params(),
        cost_estimate=cost(0, 3 * 2**20),
    )(queries, query_seg, key_seg, after)


def ring_place():
    seq = lax.axis_index("seq")
    x, core = seq // 2, lax.rem(seq, 2)
    places = [half * 2 + jnp.bitwise_xor(core, flip) for half in range(2) for flip in range(2)]
    return seq, x, places


def attend_new_kernel(segments, rows, bias, mine, theirs, after, own, peak, total, summed):
    seq, x, places = ring_place()
    refs = (mine, theirs)
    low = segments[seq * TOK]
    last = seq // 2
    first = jnp.int32(0)
    for k in range(4):
        first = first + (segments[k * 2 * TOK + 2 * TOK - 1] < low).astype(jnp.int32)
    part_rows = pl.ds(pl.multiple_of(lax.rem(seq, 4) * TOK, TOK), TOK)
    core = lax.rem(seq, 2)
    for g in range(HEADS):
        shift = lax.rem((x // 2) * 2 + g // 2 - x + 4, 4)
        flip = jnp.bitwise_xor(core, g % 2)
        block = jnp.where(flip == 0, mine[shift, part_rows, :], theirs[shift, part_rows, :])
        own[:, 0, g * HD : (g + 1) * HD] = block[:, :HD]
        own[:, 1, g * HD : (g + 1) * HD] = block[:, HD:]
    peak[...] = jnp.full(peak.shape, MASKED, jnp.float32)
    total[...] = jnp.zeros(total.shape, jnp.float32)
    summed[...] = jnp.zeros(summed.shape, jnp.float32)

    def one_pair(i, _):
        k = last - i
        where = pl.ds(pl.multiple_of(lax.rem(k, 2) * 2 * TOK, 2 * TOK), 2 * TOK)
        pieces = [
            refs[flip][lax.rem((k // 2) * 2 + half - x + 4, 4), where, :] for half in range(2) for flip in range(2)
        ]
        absorb(places, pieces, rows, None, bias[k], (peak, total, summed))
        return 0

    lax.fori_loop(0, last - first + 1, one_pair, 0)


def attend_new(segments, rows, bias, mine, theirs, after):
    return pl.pallas_call(
        attend_new_kernel,
        name="attend_new",
        out_shape=(
            bf16(TOK, 2, HEADS * HD),
            f32(HEADS, 8, ROWS),
            f32(HEADS, 8, ROWS),
            f32(HEADS, HD, ROWS),
        ),
        in_specs=[SMEM] + [VMEM] * 5,
        out_specs=(VMEM,) * 4,
        compiler_params=params(),
        cost_estimate=cost(2 * 10**9, 6 * 2**20, 3 * 10**6),
    )(segments, rows, bias, mine, theirs, after)


def attend_pages_kernel(
    requests, segments, query_seg, rows, peak_in, total_in, summed_in, mine, theirs, out, peak, total, summed, chosen
):
    seq, x, places = ring_place()
    span = lax.axis_index("cache")
    refs = (mine, theirs)
    low, high = segments[seq * TOK], segments[seq * TOK + TOK - 1]
    count = jnp.int32(0)
    for slot in range(HITS):
        chosen[count] = jnp.int32(slot)
        request = requests[span, slot]
        count = count + ((request >= low) & (request <= high)).astype(jnp.int32)
    peak[...] = peak_in[...]
    total[...] = total_in[...]
    summed[...] = summed_in[...]
    seg = query_seg[...]

    def one_pair(pair, _):
        slots = [chosen[2 * pair], chosen[jnp.minimum(2 * pair + 1, count - 1)]]
        second = jnp.where(2 * pair + 1 < count, requests[span, slots[1]], -1)
        limits = [seg == requests[span, slots[0]], seg == second]
        pieces = [
            jnp.concatenate(
                [
                    refs[flip][
                        lax.rem(2 * part + half - x + 4, 4), pl.ds(pl.multiple_of(slot * HALF, HALF), HALF), :
                    ]
                    for slot in slots
                    for part in range(2)
                ],
                axis=0,
            )
            for half in range(2)
            for flip in range(2)
        ]
        absorb(places, pieces, rows, limits, None, (peak, total, summed))
        return 0

    lax.fori_loop(0, (count + 1) // 2, one_pair, 0)
    for g in range(HEADS):
        for chunk in range(CHUNKS):
            where = slice(chunk * TOK, (chunk + 1) * TOK)
            value = summed[g, :, where] / jnp.sum(total[g, :, where], axis=0, keepdims=True)
            column = (g * GROUP + chunk % GROUP) * HD
            out[chunk // GROUP, :, column : column + HD] = jnp.transpose(value.astype(jnp.bfloat16))


def attend_pages(requests, segments, query_seg, rows, state, mine, theirs):
    return pl.pallas_call(
        attend_pages_kernel,
        name="attend_pages",
        out_shape=bf16(LAYERS, TOK, HEADS * GROUP * HD),
        in_specs=[SMEM, SMEM] + [VMEM] * 7,
        out_specs=VMEM,
        scratch_shapes=[
            pltpu.VMEM((HEADS, 8, ROWS), jnp.float32),
            pltpu.VMEM((HEADS, 8, ROWS), jnp.float32),
            pltpu.VMEM((HEADS, HD, ROWS), jnp.float32),
            pltpu.SMEM((HITS + 1,), jnp.int32),
        ],
        compiler_params=params(),
        cost_estimate=cost(3 * 10**9, 6 * 2**20, 5 * 10**6),
    )(requests, segments, query_seg, rows, *state, mine, theirs)


def seq_gather(block, *after):
    mine = relay(
        [
            block,
            lax.ppermute(block, "seq", XDOWN),
            lax.ppermute(block, "seq", XFAR),
            lax.ppermute(block, "seq", XUP),
        ],
        after,
    )
    return mine, lax.ppermute(mine, "seq", CORE)


def on_device(hidden, kv_weight, queries, kv_pool, hit_host, hit_page, hit_request, segment_ids):
    seq = lax.axis_index("seq")
    quarter = lax.rem(seq, 4)
    segments = segment_ids[0]
    query_seg = lax.dynamic_slice_in_dim(segments, seq * TOK, TOK).reshape(1, TOK)

    own_cols = lax.dynamic_slice_in_dim(kv_weight, quarter * HD, HD, 2).reshape(256, 2 * HD)
    near_cols = lax.ppermute(own_cols, "cache", CACHE_NEAR)
    hosts = hit_host[:, :, 0]
    pool = lax.dynamic_slice(
        kv_pool, (0, (seq // 4) * HALF, 0, quarter * HD), (kv_pool.shape[0], HALF, 2, HD)
    ).reshape(kv_pool.shape[0], HALF, 2 * HD)
    sent = stage(hidden[0], pool)
    both = order(own_cols, near_cols, hosts, pool)
    ups, downs = [both], [both]
    for step in range(3):
        ups.append(lax.ppermute(ups[-1], "cache", CACHE_UP))
        downs.append(lax.ppermute(downs[-1], "cache", CACHE_DOWN))
    far = lax.ppermute(ups[3], "cache", CACHE_UP)
    weights = [both, ups[1], downs[1], ups[2], downs[2], ups[3], downs[3]]

    across = lax.ppermute(hidden[0], "seq", XPAIR)
    other = lax.ppermute(sent, "head", HEAD)
    diagonal = lax.ppermute(sent, ("seq", "head"), DIAGONAL)
    hidden_mine = relay([sent, across, other, diagonal], (ups[3], downs[3]))
    hidden_theirs = lax.ppermute(hidden_mine, "seq", CORE)

    partial, far_hidden = project_near(hidden_mine, hidden_theirs, weights)
    block = project_far(partial, far_hidden, far)
    packed = pack(hosts, hit_page, pool, block)
    arrived = lax.all_to_all(packed, "cache", split_axis=0, concat_axis=0, tiled=True)
    new_mine, new_theirs = seq_gather(block)
    rows, bias = prepare(queries[:, 0], query_seg, segments.reshape(8, TOK), new_mine)

    prefix = unpack(hosts, arrived, new_theirs)
    own, *state = attend_new(segments, rows, bias, new_mine, new_theirs, prefix)
    page_mine, page_theirs = seq_gather(prefix, state[0])
    attended = attend_pages(hit_request, segments, query_seg, rows, state, page_mine, page_theirs)
    return attended[:, None], own[None]


def solution(mesh):
    return jax.shard_map(
        on_device,
        mesh=mesh,
        in_specs=(
            P("cache", "seq", "head"),
            P("cache", None, "head"),
            P(None, "cache", "seq", "head"),
            P("cache", None, None, "head"),
            P(),
            P(),
            P(),
            P("cache", None),
        ),
        out_specs=(P(None, "cache", "seq", "head"), P("cache", "seq", None, "head")),
        check_vma=False,
    )
```

```python
import math

import jax
import jax.numpy as jnp
from jax import lax
from jax.experimental import pallas as pl
from jax.experimental.pallas import tpu as pltpu
from jax.sharding import PartitionSpec as P

HD = 128
CAP = 2
HEADS = 4
GROUP = 4
TOK = 128
LAYERS = 2
CHUNKS = LAYERS * GROUP
ROWS = CHUNKS * TOK
WIDTH = 1024
HITS = 11
HALF = 64
SPANS = 16
MASKED = -1e30
NEVER = 1e30
FACTOR = math.log2(math.e) / math.sqrt(HD)
VMEM_LIMIT = 16 * 1024 * 1024

CACHE_UP = [(i, (i + 2) % 16) for i in range(16)]
CACHE_DOWN = [(i, (i - 2) % 16) for i in range(16)]
CACHE_NEAR = [(i, i ^ 1) for i in range(16)]
CORE = [(i, i ^ 1) for i in range(8)]
XPAIR = [(i, i ^ 2) for i in range(8)]
XUP = [(i, (i + 2) % 8) for i in range(8)]
XDOWN = [(i, (i - 2) % 8) for i in range(8)]
XFAR = [(i, (i + 4) % 8) for i in range(8)]
HEAD = [(0, 1), (1, 0)]
DIAGONAL = [(i, i ^ 5) for i in range(16)]
ANY = pl.BlockSpec(memory_space=pl.ANY)
SMEM = pl.BlockSpec(memory_space=pltpu.SMEM)
VMEM = pl.BlockSpec(memory_space=pltpu.VMEM)


def params():
    return pltpu.CompilerParams(vmem_limit_bytes=VMEM_LIMIT)


def cost(flops, transferred, exps=0):
    return pl.CostEstimate(flops=flops, bytes_accessed=transferred, transcendentals=exps)


def bf16(*shape):
    return jax.ShapeDtypeStruct(shape, jnp.bfloat16)


def f32(*shape):
    return jax.ShapeDtypeStruct(shape, jnp.float32)


def pack_kernel(hosts, pages, pool, *refs):
    out = refs[-1]
    me = lax.axis_index("cache")

    def one_span(c, _):
        found, first, second = jnp.int32(0), jnp.int32(0), jnp.int32(0)
        for h in range(HITS):
            here = hosts[c, h] == me
            page = pages[c, h]
            first = jnp.where(here & (found == 0), page, first)
            second = jnp.where(here & (found == 1), page, second)
            found = found + here.astype(jnp.int32)
        out[c * CAP] = pool[first]
        out[c * CAP + 1] = pool[second]
        return 0

    lax.fori_loop(0, SPANS, one_span, 0)


def pack(hosts, pages, pool, *after):
    return pl.pallas_call(
        pack_kernel,
        name="pack",
        out_shape=bf16(SPANS * CAP, HALF, 2 * HD),
        in_specs=[SMEM, SMEM, VMEM] + [VMEM] * len(after),
        out_specs=VMEM,
        compiler_params=params(),
        cost_estimate=cost(0, 2 * 2**20),
    )(hosts, pages, pool, *after)


def unpack_kernel(hosts, arrived, after, out):
    me = lax.axis_index("cache")
    for h in range(HITS):
        host = hosts[me, h]
        place = host * CAP
        for other in range(h):
            place = place + (hosts[me, other] == host).astype(jnp.int32)
        out[h * HALF : (h + 1) * HALF] = arrived[place]


def unpack(hosts, arrived, after):
    return pl.pallas_call(
        unpack_kernel,
        name="unpack",
        out_shape=bf16(HITS * HALF, 2 * HD),
        in_specs=[SMEM, VMEM, ANY],
        out_specs=VMEM,
        compiler_params=params(),
        cost_estimate=cost(0, 2**20),
    )(hosts, arrived, after)


def project_near_kernel(mine, theirs, *refs):
    weights = refs[:7]
    partial, far_hidden, hid, wts = refs[-4:]
    head = lax.axis_index("head")
    quarter = lax.rem(lax.axis_index("seq"), 4)
    z = lax.axis_index("cache") // 2
    far = pl.multiple_of(lax.rem(z + 4, 8) * 512, 512)
    for i in range(4):
        columns = pl.multiple_of(jnp.bitwise_xor(head, i // 2) * 2048, 2048)
        for flip, block in enumerate((mine, theirs)):
            tokens = pl.multiple_of(jnp.bitwise_xor(quarter, 2 * (i % 2) + flip) * TOK, TOK)
            hid[pl.ds(tokens, TOK), pl.ds(columns, 2048)] = block[i]
    for i, shift in enumerate((0, -1, 1, -2, 2, -3, 3)):
        row = pl.multiple_of(lax.rem(z + shift + 8, 8) * 512, 512)
        wts[pl.ds(row, 512)] = weights[i][...]
    wts[pl.ds(far, 512)] = jnp.zeros((512, 2 * HD), jnp.bfloat16)
    partial[...] = jnp.dot(hid[...], wts[...], preferred_element_type=jnp.float32)
    far_hidden[...] = hid[:, pl.ds(far, 512)]


def project_near(mine, theirs, weights):
    return pl.pallas_call(
        project_near_kernel,
        name="project_near",
        out_shape=(f32(4 * TOK, 2 * HD), bf16(4 * TOK, 512)),
        in_specs=[VMEM] * 9,
        out_specs=(VMEM, VMEM),
        scratch_shapes=[
            pltpu.VMEM((4 * TOK, 4096), jnp.bfloat16),
            pltpu.VMEM((4096, 2 * HD), jnp.bfloat16),
        ],
        compiler_params=params(),
        cost_estimate=cost(2 * 512 * 3584 * 256, 6 * 2**20),
    )(mine, theirs, *weights)


def project_far_kernel(partial, far_hidden, weights, out):
    out[...] = (
        partial[...] + jnp.dot(far_hidden[...], weights[...], preferred_element_type=jnp.float32)
    ).astype(out.dtype)


def project_far(partial, far_hidden, weights):
    return pl.pallas_call(
        project_far_kernel,
        name="project_far",
        out_shape=bf16(4 * TOK, 2 * HD),
        in_specs=[VMEM] * 3,
        out_specs=VMEM,
        compiler_params=params(),
        cost_estimate=cost(2 * 512 * 512 * 256, 2**20),
    )(partial, far_hidden, weights)


def absorb(places, pieces, rows, limits, bias, state):
    peaks, totals, sums = state
    steps = [(g, part) for g in range(HEADS) for part in range(ROWS // WIDTH)]
    repeat = WIDTH // TOK
    wide = None if limits is None else [jnp.concatenate([limit] * repeat, axis=1) for limit in limits]
    if bias is not None:
        bias = jnp.concatenate([bias] * repeat, axis=1)
    flipped = [jnp.transpose(piece[:, HD:]) for piece in pieces]

    def raw(i):
        g, part = steps[i]
        place = places[g]
        return jnp.dot(
            pieces[g][:, :HD], rows[place, :, part * WIDTH : (part + 1) * WIDTH], preferred_element_type=jnp.float32
        )

    def soften(i, found):
        g, part = steps[i]
        place = places[g]
        where = slice(part * WIDTH, (part + 1) * WIDTH)
        scaled = found * FACTOR
        if bias is not None:
            scaled = scaled + bias
        halves = scaled.shape[0] // TOK
        largest = None
        for h in range(halves):
            block = jnp.max(scaled[h * TOK : (h + 1) * TOK].reshape(TOK // 8, 8, WIDTH), axis=0)
            if wide is not None:
                block = jnp.where(wide[h], block, MASKED)
            largest = block if largest is None else jnp.maximum(largest, block)
        before = peaks[place, 0:1, where]
        peak = jnp.maximum(before, jnp.max(largest, axis=0, keepdims=True))
        shrink = jnp.exp2(before - peak)
        probs = []
        for h in range(halves):
            level = peak if wide is None else jnp.where(wide[h], peak, NEVER)
            probs.append(jnp.exp2(scaled[h * TOK : (h + 1) * TOK] - level))
        total = totals[place, :, where] * shrink
        for block in probs:
            total = total + jnp.sum(block.reshape(TOK // 8, 8, WIDTH), axis=0)
        peaks[place, 0:1, where] = peak
        totals[place, :, where] = total
        return jnp.concatenate([block.astype(jnp.bfloat16) for block in probs], axis=0), shrink

    def add(i, probs, shrink):
        g, part = steps[i]
        place = places[g]
        where = slice(part * WIDTH, (part + 1) * WIDTH)
        sums[place, :, where] = sums[place, :, where] * shrink + jnp.dot(
            flipped[g], probs, preferred_element_type=jnp.float32
        )

    found, held = raw(0), None
    for i in range(len(steps)):
        following = raw(i + 1) if i + 1 < len(steps) else None
        if held is not None:
            add(i - 1, *held)
        held = soften(i, found)
        found = following
    add(len(steps) - 1, *held)


def hold_kernel(*refs):
    pass


def hold(array, *after):
    return pl.pallas_call(
        hold_kernel,
        name="hold",
        out_shape=bf16(*array.shape),
        in_specs=[ANY] * (1 + len(after)),
        out_specs=ANY,
        input_output_aliases={0: 0},
        compiler_params=params(),
        cost_estimate=cost(0, 1),
    )(array, *after)


def relay_kernel(*refs):
    out = refs[-1]
    for i in range(4):
        out[i] = refs[i][...]


def relay(blocks, after, late=()):
    return pl.pallas_call(
        relay_kernel,
        name="relay",
        out_shape=bf16(4, *blocks[0].shape),
        in_specs=[VMEM] * 4 + [VMEM] * len(after) + [ANY] * len(late),
        out_specs=VMEM,
        compiler_params=params(),
        cost_estimate=cost(0, 2**21),
    )(*blocks, *after, *late)


def stage_kernel(hidden, pool, sent):
    sent[...] = hidden[...]


def stage(hidden, pool):
    return pl.pallas_call(
        stage_kernel,
        name="stage",
        out_shape=bf16(*hidden.shape),
        in_specs=[VMEM, VMEM],
        out_specs=VMEM,
        compiler_params=params(),
        cost_estimate=cost(0, 2**20),
    )(hidden, pool)


def order_kernel(own_cols, near_cols, hosts, pool, both):
    odd = lax.rem(lax.axis_index("cache"), 2)
    both[pl.ds(pl.multiple_of(odd * 256, 256), 256)] = own_cols[...]
    both[pl.ds(pl.multiple_of(256 - odd * 256, 256), 256)] = near_cols[...]


def order(own_cols, near_cols, hosts, pool):
    return pl.pallas_call(
        order_kernel,
        name="order",
        out_shape=bf16(512, 2 * HD),
        in_specs=[VMEM, VMEM, SMEM, VMEM],
        out_specs=VMEM,
        compiler_params=params(),
        cost_estimate=cost(0, 2**19),
    )(own_cols, near_cols, hosts, pool)


def prepare_kernel(queries, query_seg, key_seg, after, rows, bias):
    seq = lax.axis_index("seq")
    for g in range(HEADS):
        for chunk in range(CHUNKS):
            column = (g * GROUP + chunk % GROUP) * HD
            rows[g, :, chunk * TOK : (chunk + 1) * TOK] = jnp.transpose(
                queries[chunk // GROUP, :, column : column + HD]
            )
    query_wide = jnp.broadcast_to(query_seg[...], (TOK, TOK))
    key_row = lax.broadcasted_iota(jnp.int32, (TOK, TOK), 0)
    query_lane = lax.broadcasted_iota(jnp.int32, (TOK, TOK), 1) + seq * TOK
    for block in range(8):
        key_wide = jnp.transpose(jnp.broadcast_to(key_seg[block : block + 1], (TOK, TOK)))
        allowed = (key_wide == query_wide) & (key_row + block * TOK <= query_lane)
        bias[block // 2, (block % 2) * TOK : (block % 2 + 1) * TOK] = jnp.where(allowed, 0.0, MASKED)


def prepare(queries, query_seg, key_seg, after):
    return pl.pallas_call(
        prepare_kernel,
        name="prepare",
        out_shape=(bf16(HEADS, HD, ROWS), f32(4, 2 * TOK, TOK)),
        in_specs=[VMEM] * 4,
        out_specs=(VMEM,) * 2,
        compiler_params=params(),
        cost_estimate=cost(0, 3 * 2**20),
    )(queries, query_seg, key_seg, after)


def ring_place():
    seq = lax.axis_index("seq")
    x, core = seq // 2, lax.rem(seq, 2)
    places = [half * 2 + jnp.bitwise_xor(core, flip) for half in range(2) for flip in range(2)]
    return seq, x, places


def attend_new_kernel(segments, rows, bias, mine, far_theirs, after, own, peak, total, summed, theirs, sem):
    copy = pltpu.make_async_copy(far_theirs, theirs, sem)
    copy.start()
    seq, x, places = ring_place()
    refs = (mine, theirs)
    low = segments[seq * TOK]
    last = seq // 2
    first = jnp.int32(0)
    for k in range(4):
        first = first + (segments[k * 2 * TOK + 2 * TOK - 1] < low).astype(jnp.int32)
    part_rows = pl.ds(pl.multiple_of(lax.rem(seq, 4) * TOK, TOK), TOK)
    core = lax.rem(seq, 2)
    copy.wait()
    for g in range(HEADS):
        shift = lax.rem((x // 2) * 2 + g // 2 - x + 4, 4)
        flip = jnp.bitwise_xor(core, g % 2)
        block = jnp.where(flip == 0, mine[shift, part_rows, :], theirs[shift, part_rows, :])
        own[:, 0, g * HD : (g + 1) * HD] = block[:, :HD]
        own[:, 1, g * HD : (g + 1) * HD] = block[:, HD:]
    peak[...] = jnp.full(peak.shape, MASKED, jnp.float32)
    total[...] = jnp.zeros(total.shape, jnp.float32)
    summed[...] = jnp.zeros(summed.shape, jnp.float32)

    def one_pair(i, _):
        k = last - i
        where = pl.ds(pl.multiple_of(lax.rem(k, 2) * 2 * TOK, 2 * TOK), 2 * TOK)
        pieces = [
            refs[flip][lax.rem((k // 2) * 2 + half - x + 4, 4), where, :] for half in range(2) for flip in range(2)
        ]
        absorb(places, pieces, rows, None, bias[k], (peak, total, summed))
        return 0

    lax.fori_loop(0, last - first + 1, one_pair, 0)


def attend_new(segments, rows, bias, mine, theirs, after):
    return pl.pallas_call(
        attend_new_kernel,
        name="attend_new",
        out_shape=(
            bf16(TOK, 2, HEADS * HD),
            f32(HEADS, 8, ROWS),
            f32(HEADS, 8, ROWS),
            f32(HEADS, HD, ROWS),
        ),
        in_specs=[SMEM] + [VMEM] * 3 + [ANY, VMEM],
        out_specs=(VMEM,) * 4,
        scratch_shapes=[pltpu.VMEM((4, 4 * TOK, 2 * HD), jnp.bfloat16), pltpu.SemaphoreType.DMA],
        compiler_params=params(),
        cost_estimate=cost(2 * 10**9, 6 * 2**20, 3 * 10**6),
    )(segments, rows, bias, mine, theirs, after)


def attend_pages_kernel(
    requests, segments, query_seg, rows, peak_in, total_in, summed_in, mine, theirs, out, peak, total, summed, chosen
):
    seq, x, places = ring_place()
    span = lax.axis_index("cache")
    refs = (mine, theirs)
    low, high = segments[seq * TOK], segments[seq * TOK + TOK - 1]
    count = jnp.int32(0)
    for slot in range(HITS):
        chosen[count] = jnp.int32(slot)
        request = requests[span, slot]
        count = count + ((request >= low) & (request <= high)).astype(jnp.int32)
    peak[...] = peak_in[...]
    total[...] = total_in[...]
    summed[...] = summed_in[...]
    seg = query_seg[...]

    def one_pair(pair, _):
        slots = [chosen[2 * pair], chosen[jnp.minimum(2 * pair + 1, count - 1)]]
        second = jnp.where(2 * pair + 1 < count, requests[span, slots[1]], -1)
        limits = [seg == requests[span, slots[0]], seg == second]
        pieces = [
            jnp.concatenate(
                [
                    refs[flip][
                        lax.rem(2 * part + half - x + 4, 4), pl.ds(pl.multiple_of(slot * HALF, HALF), HALF), :
                    ]
                    for slot in slots
                    for part in range(2)
                ],
                axis=0,
            )
            for half in range(2)
            for flip in range(2)
        ]
        absorb(places, pieces, rows, limits, None, (peak, total, summed))
        return 0

    lax.fori_loop(0, (count + 1) // 2, one_pair, 0)
    for g in range(HEADS):
        for chunk in range(CHUNKS):
            where = slice(chunk * TOK, (chunk + 1) * TOK)
            value = summed[g, :, where] / jnp.sum(total[g, :, where], axis=0, keepdims=True)
            column = (g * GROUP + chunk % GROUP) * HD
            out[chunk // GROUP, :, column : column + HD] = jnp.transpose(value.astype(jnp.bfloat16))


def attend_pages(requests, segments, query_seg, rows, state, mine, theirs):
    return pl.pallas_call(
        attend_pages_kernel,
        name="attend_pages",
        out_shape=bf16(LAYERS, TOK, HEADS * GROUP * HD),
        in_specs=[SMEM, SMEM] + [VMEM] * 7,
        out_specs=VMEM,
        scratch_shapes=[
            pltpu.VMEM((HEADS, 8, ROWS), jnp.float32),
            pltpu.VMEM((HEADS, 8, ROWS), jnp.float32),
            pltpu.VMEM((HEADS, HD, ROWS), jnp.float32),
            pltpu.SMEM((HITS + 1,), jnp.int32),
        ],
        compiler_params=params(),
        cost_estimate=cost(3 * 10**9, 6 * 2**20, 5 * 10**6),
    )(requests, segments, query_seg, rows, *state, mine, theirs)


def seq_gather(block, *after):
    mine = relay(
        [
            block,
            lax.ppermute(block, "seq", XDOWN),
            lax.ppermute(block, "seq", XFAR),
            lax.ppermute(block, "seq", XUP),
        ],
        after,
    )
    return mine, lax.ppermute(mine, "seq", CORE)


def on_device(hidden, kv_weight, queries, kv_pool, hit_host, hit_page, hit_request, segment_ids):
    seq = lax.axis_index("seq")
    quarter = lax.rem(seq, 4)
    segments = segment_ids[0]
    query_seg = lax.dynamic_slice_in_dim(segments, seq * TOK, TOK).reshape(1, TOK)

    own_cols = lax.dynamic_slice_in_dim(kv_weight, quarter * HD, HD, 2).reshape(256, 2 * HD)
    near_cols = lax.ppermute(own_cols, "cache", CACHE_NEAR)
    hosts = hit_host[:, :, 0]
    pool = lax.dynamic_slice(
        kv_pool, (0, (seq // 4) * HALF, 0, quarter * HD), (kv_pool.shape[0], HALF, 2, HD)
    ).reshape(kv_pool.shape[0], HALF, 2 * HD)
    sent = stage(hidden[0], pool)
    both = order(own_cols, near_cols, hosts, pool)
    ups, downs = [both], [both]
    for step in range(3):
        ups.append(lax.ppermute(ups[-1], "cache", CACHE_UP))
        downs.append(lax.ppermute(downs[-1], "cache", CACHE_DOWN))
    far = lax.ppermute(ups[3], "cache", CACHE_UP)
    weights = [both, ups[1], downs[1], ups[2], downs[2], ups[3], downs[3]]

    across = lax.ppermute(hidden[0], "seq", XPAIR)
    other = lax.ppermute(sent, "head", HEAD)
    diagonal = lax.ppermute(sent, ("seq", "head"), DIAGONAL)
    packed = pack(hosts, hit_page, pool, ups[1])
    hidden_mine = relay([sent, across, other, diagonal], (ups[3], downs[3]), (packed,))
    hidden_theirs = lax.ppermute(hidden_mine, "seq", CORE)

    partial, far_hidden = project_near(hidden_mine, hidden_theirs, weights)
    block = project_far(partial, far_hidden, far)
    arrived = lax.all_to_all(hold(packed, block), "cache", split_axis=0, concat_axis=0, tiled=True)
    new_mine, new_theirs = seq_gather(block)
    rows, bias = prepare(queries[:, 0], query_seg, segments.reshape(8, TOK), new_mine)

    prefix = unpack(hosts, arrived, new_theirs)
    own, *state = attend_new(segments, rows, bias, new_mine, new_theirs, prefix)
    page_mine, page_theirs = seq_gather(prefix, state[0])
    attended = attend_pages(hit_request, segments, query_seg, rows, state, page_mine, page_theirs)
    return attended[:, None], own[None]


def solution(mesh):
    return jax.shard_map(
        on_device,
        mesh=mesh,
        in_specs=(
            P("cache", "seq", "head"),
            P("cache", None, "head"),
            P(None, "cache", "seq", "head"),
            P("cache", None, None, "head"),
            P(),
            P(),
            P(),
            P("cache", None),
        ),
        out_specs=(P(None, "cache", "seq", "head"), P("cache", "seq", None, "head")),
        check_vma=False,
    )
```

```python
import math

import jax
import jax.numpy as jnp
from jax import lax
from jax.experimental import pallas as pl
from jax.experimental.pallas import tpu as pltpu
from jax.sharding import PartitionSpec as P

HD = 128
CAP = 2
HEADS = 4
GROUP = 4
TOK = 128
LAYERS = 2
CHUNKS = LAYERS * GROUP
ROWS = CHUNKS * TOK
WIDTH = 1024
HITS = 11
HALF = 64
SPANS = 16
MASKED = -1e30
NEVER = 1e30
FACTOR = math.log2(math.e) / math.sqrt(HD)
VMEM_LIMIT = 16 * 1024 * 1024

CACHE_UP = [(i, (i + 2) % 16) for i in range(16)]
CACHE_DOWN = [(i, (i - 2) % 16) for i in range(16)]
CACHE_NEAR = [(i, i ^ 1) for i in range(16)]
CORE = [(i, i ^ 1) for i in range(8)]
XPAIR = [(i, i ^ 2) for i in range(8)]
XUP = [(i, (i + 2) % 8) for i in range(8)]
XDOWN = [(i, (i - 2) % 8) for i in range(8)]
XFAR = [(i, (i + 4) % 8) for i in range(8)]
HEAD = [(0, 1), (1, 0)]
DIAGONAL = [(i, i ^ 5) for i in range(16)]
ANY = pl.BlockSpec(memory_space=pl.ANY)
SMEM = pl.BlockSpec(memory_space=pltpu.SMEM)
VMEM = pl.BlockSpec(memory_space=pltpu.VMEM)


def params():
    return pltpu.CompilerParams(vmem_limit_bytes=VMEM_LIMIT)


def cost(flops, transferred, exps=0):
    return pl.CostEstimate(flops=flops, bytes_accessed=transferred, transcendentals=exps)


def bf16(*shape):
    return jax.ShapeDtypeStruct(shape, jnp.bfloat16)


def f32(*shape):
    return jax.ShapeDtypeStruct(shape, jnp.float32)


def pack_kernel(hosts, pages, pool, *refs):
    out = refs[-1]
    me = lax.axis_index("cache")

    def one_span(c, _):
        found, first, second = jnp.int32(0), jnp.int32(0), jnp.int32(0)
        for h in range(HITS):
            here = hosts[c, h] == me
            page = pages[c, h]
            first = jnp.where(here & (found == 0), page, first)
            second = jnp.where(here & (found == 1), page, second)
            found = found + here.astype(jnp.int32)
        out[c * CAP] = pool[first]
        out[c * CAP + 1] = pool[second]
        return 0

    lax.fori_loop(0, SPANS, one_span, 0)


def pack(hosts, pages, pool, *after):
    return pl.pallas_call(
        pack_kernel,
        name="pack",
        out_shape=bf16(SPANS * CAP, HALF, 2 * HD),
        in_specs=[SMEM, SMEM, VMEM] + [VMEM] * len(after),
        out_specs=VMEM,
        compiler_params=params(),
        cost_estimate=cost(0, 2 * 2**20),
    )(hosts, pages, pool, *after)


def unpack_kernel(hosts, arrived, after, out):
    me = lax.axis_index("cache")
    for h in range(HITS):
        host = hosts[me, h]
        place = host * CAP
        for other in range(h):
            place = place + (hosts[me, other] == host).astype(jnp.int32)
        out[h * HALF : (h + 1) * HALF] = arrived[place]


def unpack(hosts, arrived, after):
    return pl.pallas_call(
        unpack_kernel,
        name="unpack",
        out_shape=bf16(HITS * HALF, 2 * HD),
        in_specs=[SMEM, VMEM, ANY],
        out_specs=VMEM,
        compiler_params=params(),
        cost_estimate=cost(0, 2**20),
    )(hosts, arrived, after)


def project_near_kernel(mine, theirs, *refs):
    weights = refs[:7]
    partial, far_hidden, hid, wts = refs[-4:]
    head = lax.axis_index("head")
    quarter = lax.rem(lax.axis_index("seq"), 4)
    z = lax.axis_index("cache") // 2
    far = pl.multiple_of(lax.rem(z + 4, 8) * 512, 512)
    for i in range(4):
        columns = pl.multiple_of(jnp.bitwise_xor(head, i // 2) * 2048, 2048)
        for flip, block in enumerate((mine, theirs)):
            tokens = pl.multiple_of(jnp.bitwise_xor(quarter, 2 * (i % 2) + flip) * TOK, TOK)
            hid[pl.ds(tokens, TOK), pl.ds(columns, 2048)] = block[i]
    for i, shift in enumerate((0, -1, 1, -2, 2, -3, 3)):
        row = pl.multiple_of(lax.rem(z + shift + 8, 8) * 512, 512)
        wts[pl.ds(row, 512)] = weights[i][...]
    wts[pl.ds(far, 512)] = jnp.zeros((512, 2 * HD), jnp.bfloat16)
    partial[...] = jnp.dot(hid[...], wts[...], preferred_element_type=jnp.float32)
    far_hidden[...] = hid[:, pl.ds(far, 512)]


def project_near(mine, theirs, weights):
    return pl.pallas_call(
        project_near_kernel,
        name="project_near",
        out_shape=(f32(4 * TOK, 2 * HD), bf16(4 * TOK, 512)),
        in_specs=[VMEM] * 9,
        out_specs=(VMEM, VMEM),
        scratch_shapes=[
            pltpu.VMEM((4 * TOK, 4096), jnp.bfloat16),
            pltpu.VMEM((4096, 2 * HD), jnp.bfloat16),
        ],
        compiler_params=params(),
        cost_estimate=cost(2 * 512 * 3584 * 256, 6 * 2**20),
    )(mine, theirs, *weights)


def project_far_kernel(partial, far_hidden, weights_a, weights_b, out):
    out[...] = (
        partial[...]
        + jnp.dot(far_hidden[:, :256], weights_a[...], preferred_element_type=jnp.float32)
        + jnp.dot(far_hidden[:, 256:], weights_b[...], preferred_element_type=jnp.float32)
    ).astype(out.dtype)


def project_far(partial, far_hidden, weights_a, weights_b):
    return pl.pallas_call(
        project_far_kernel,
        name="project_far",
        out_shape=bf16(4 * TOK, 2 * HD),
        in_specs=[VMEM] * 4,
        out_specs=VMEM,
        compiler_params=params(),
        cost_estimate=cost(2 * 512 * 512 * 256, 2**20),
    )(partial, far_hidden, weights_a, weights_b)


def absorb(places, pieces, rows, limits, bias, state):
    peaks, totals, sums = state
    steps = [(g, part) for g in range(HEADS) for part in range(ROWS // WIDTH)]
    repeat = WIDTH // TOK
    wide = None if limits is None else [jnp.concatenate([limit] * repeat, axis=1) for limit in limits]
    if bias is not None:
        bias = jnp.concatenate([bias] * repeat, axis=1)
    flipped = [jnp.transpose(piece[:, HD:]) for piece in pieces]

    def raw(i):
        g, part = steps[i]
        place = places[g]
        return jnp.dot(
            pieces[g][:, :HD], rows[place, :, part * WIDTH : (part + 1) * WIDTH], preferred_element_type=jnp.float32
        )

    def soften(i, found):
        g, part = steps[i]
        place = places[g]
        where = slice(part * WIDTH, (part + 1) * WIDTH)
        scaled = found * FACTOR
        if bias is not None:
            scaled = scaled + bias
        halves = scaled.shape[0] // TOK
        largest = None
        for h in range(halves):
            block = jnp.max(scaled[h * TOK : (h + 1) * TOK].reshape(TOK // 8, 8, WIDTH), axis=0)
            if wide is not None:
                block = jnp.where(wide[h], block, MASKED)
            largest = block if largest is None else jnp.maximum(largest, block)
        before = peaks[place, 0:1, where]
        peak = jnp.maximum(before, jnp.max(largest, axis=0, keepdims=True))
        shrink = jnp.exp2(before - peak)
        probs = []
        for h in range(halves):
            level = peak if wide is None else jnp.where(wide[h], peak, NEVER)
            probs.append(jnp.exp2(scaled[h * TOK : (h + 1) * TOK] - level))
        total = totals[place, :, where] * shrink
        for block in probs:
            total = total + jnp.sum(block.reshape(TOK // 8, 8, WIDTH), axis=0)
        peaks[place, 0:1, where] = peak
        totals[place, :, where] = total
        return jnp.concatenate([block.astype(jnp.bfloat16) for block in probs], axis=0), shrink

    def add(i, probs, shrink):
        g, part = steps[i]
        place = places[g]
        where = slice(part * WIDTH, (part + 1) * WIDTH)
        sums[place, :, where] = sums[place, :, where] * shrink + jnp.dot(
            flipped[g], probs, preferred_element_type=jnp.float32
        )

    found, held = raw(0), None
    for i in range(len(steps)):
        following = raw(i + 1) if i + 1 < len(steps) else None
        if held is not None:
            add(i - 1, *held)
        held = soften(i, found)
        found = following
    add(len(steps) - 1, *held)


def hold_kernel(*refs):
    pass


def hold(array, *after):
    return pl.pallas_call(
        hold_kernel,
        name="hold",
        out_shape=bf16(*array.shape),
        in_specs=[ANY] * (1 + len(after)),
        out_specs=ANY,
        input_output_aliases={0: 0},
        compiler_params=params(),
        cost_estimate=cost(0, 1),
    )(array, *after)


def relay_kernel(*refs):
    out = refs[-1]
    for i in range(4):
        out[i] = refs[i][...]


def relay(blocks, after):
    return pl.pallas_call(
        relay_kernel,
        name="relay",
        out_shape=bf16(4, *blocks[0].shape),
        in_specs=[VMEM] * (4 + len(after)),
        out_specs=VMEM,
        compiler_params=params(),
        cost_estimate=cost(0, 2**21),
    )(*blocks, *after)


def stage_kernel(hidden, pool, sent):
    sent[...] = hidden[...]


def stage(hidden, pool):
    return pl.pallas_call(
        stage_kernel,
        name="stage",
        out_shape=bf16(*hidden.shape),
        in_specs=[VMEM, VMEM],
        out_specs=VMEM,
        compiler_params=params(),
        cost_estimate=cost(0, 2**20),
    )(hidden, pool)


def order_kernel(own_cols, near_cols, hosts, pool, both):
    odd = lax.rem(lax.axis_index("cache"), 2)
    both[pl.ds(pl.multiple_of(odd * 256, 256), 256)] = own_cols[...]
    both[pl.ds(pl.multiple_of(256 - odd * 256, 256), 256)] = near_cols[...]


def order(own_cols, near_cols, hosts, pool):
    return pl.pallas_call(
        order_kernel,
        name="order",
        out_shape=bf16(512, 2 * HD),
        in_specs=[VMEM, VMEM, SMEM, VMEM],
        out_specs=VMEM,
        compiler_params=params(),
        cost_estimate=cost(0, 2**19),
    )(own_cols, near_cols, hosts, pool)


def prepare_kernel(queries, query_seg, key_seg, after, rows, bias):
    seq = lax.axis_index("seq")
    for g in range(HEADS):
        for chunk in range(CHUNKS):
            column = (g * GROUP + chunk % GROUP) * HD
            rows[g, :, chunk * TOK : (chunk + 1) * TOK] = jnp.transpose(
                queries[chunk // GROUP, :, column : column + HD]
            )
    query_wide = jnp.broadcast_to(query_seg[...], (TOK, TOK))
    key_row = lax.broadcasted_iota(jnp.int32, (TOK, TOK), 0)
    query_lane = lax.broadcasted_iota(jnp.int32, (TOK, TOK), 1) + seq * TOK
    for block in range(8):
        key_wide = jnp.transpose(jnp.broadcast_to(key_seg[block : block + 1], (TOK, TOK)))
        allowed = (key_wide == query_wide) & (key_row + block * TOK <= query_lane)
        bias[block // 2, (block % 2) * TOK : (block % 2 + 1) * TOK] = jnp.where(allowed, 0.0, MASKED)


def prepare(queries, query_seg, key_seg, after):
    return pl.pallas_call(
        prepare_kernel,
        name="prepare",
        out_shape=(bf16(HEADS, HD, ROWS), f32(4, 2 * TOK, TOK)),
        in_specs=[VMEM] * 4,
        out_specs=(VMEM,) * 2,
        compiler_params=params(),
        cost_estimate=cost(0, 3 * 2**20),
    )(queries, query_seg, key_seg, after)


def bundle_kernel(sent, across, other, diagonal, up, down, packed, out, half_up, half_down):
    for i, block in enumerate((sent, across, other, diagonal)):
        out[i] = block[...]
    half_up[...] = up[:256]
    half_down[...] = down[256:]


def bundle(blocks, up, down, packed):
    return pl.pallas_call(
        bundle_kernel,
        name="bundle",
        out_shape=(bf16(4, *blocks[0].shape), bf16(256, 2 * HD), bf16(256, 2 * HD)),
        in_specs=[VMEM] * 6 + [ANY],
        out_specs=(VMEM,) * 3,
        compiler_params=params(),
        cost_estimate=cost(0, 2**21),
    )(*blocks, up, down, packed)


def ring_place():
    seq = lax.axis_index("seq")
    x, core = seq // 2, lax.rem(seq, 2)
    places = [half * 2 + jnp.bitwise_xor(core, flip) for half in range(2) for flip in range(2)]
    return seq, x, places


def attend_new_kernel(segments, rows, bias, mine, far_theirs, after, own, peak, total, summed, theirs, sem):
    copy = pltpu.make_async_copy(far_theirs, theirs, sem)
    copy.start()
    seq, x, places = ring_place()
    refs = (mine, theirs)
    low = segments[seq * TOK]
    last = seq // 2
    first = jnp.int32(0)
    for k in range(4):
        first = first + (segments[k * 2 * TOK + 2 * TOK - 1] < low).astype(jnp.int32)
    part_rows = pl.ds(pl.multiple_of(lax.rem(seq, 4) * TOK, TOK), TOK)
    core = lax.rem(seq, 2)
    copy.wait()
    for g in range(HEADS):
        shift = lax.rem((x // 2) * 2 + g // 2 - x + 4, 4)
        flip = jnp.bitwise_xor(core, g % 2)
        block = jnp.where(flip == 0, mine[shift, part_rows, :], theirs[shift, part_rows, :])
        own[:, 0, g * HD : (g + 1) * HD] = block[:, :HD]
        own[:, 1, g * HD : (g + 1) * HD] = block[:, HD:]
    peak[...] = jnp.full(peak.shape, MASKED, jnp.float32)
    total[...] = jnp.zeros(total.shape, jnp.float32)
    summed[...] = jnp.zeros(summed.shape, jnp.float32)

    def one_pair(i, _):
        k = last - i
        where = pl.ds(pl.multiple_of(lax.rem(k, 2) * 2 * TOK, 2 * TOK), 2 * TOK)
        pieces = [
            refs[flip][lax.rem((k // 2) * 2 + half - x + 4, 4), where, :] for half in range(2) for flip in range(2)
        ]
        absorb(places, pieces, rows, None, bias[k], (peak, total, summed))
        return 0

    lax.fori_loop(0, last - first + 1, one_pair, 0)


def attend_new(segments, rows, bias, mine, theirs, after):
    return pl.pallas_call(
        attend_new_kernel,
        name="attend_new",
        out_shape=(
            bf16(TOK, 2, HEADS * HD),
            f32(HEADS, 8, ROWS),
            f32(HEADS, 8, ROWS),
            f32(HEADS, HD, ROWS),
        ),
        in_specs=[SMEM] + [VMEM] * 3 + [ANY, VMEM],
        out_specs=(VMEM,) * 4,
        scratch_shapes=[pltpu.VMEM((4, 4 * TOK, 2 * HD), jnp.bfloat16), pltpu.SemaphoreType.DMA],
        compiler_params=params(),
        cost_estimate=cost(2 * 10**9, 6 * 2**20, 3 * 10**6),
    )(segments, rows, bias, mine, theirs, after)


def attend_pages_kernel(
    requests, segments, query_seg, rows, peak_in, total_in, summed_in, mine, theirs, out, peak, total, summed, chosen
):
    seq, x, places = ring_place()
    span = lax.axis_index("cache")
    refs = (mine, theirs)
    low, high = segments[seq * TOK], segments[seq * TOK + TOK - 1]
    count = jnp.int32(0)
    for slot in range(HITS):
        chosen[count] = jnp.int32(slot)
        request = requests[span, slot]
        count = count + ((request >= low) & (request <= high)).astype(jnp.int32)
    peak[...] = peak_in[...]
    total[...] = total_in[...]
    summed[...] = summed_in[...]
    seg = query_seg[...]

    def one_pair(pair, _):
        slots = [chosen[2 * pair], chosen[jnp.minimum(2 * pair + 1, count - 1)]]
        second = jnp.where(2 * pair + 1 < count, requests[span, slots[1]], -1)
        limits = [seg == requests[span, slots[0]], seg == second]
        pieces = [
            jnp.concatenate(
                [
                    refs[flip][
                        lax.rem(2 * part + half - x + 4, 4), pl.ds(pl.multiple_of(slot * HALF, HALF), HALF), :
                    ]
                    for slot in slots
                    for part in range(2)
                ],
                axis=0,
            )
            for half in range(2)
            for flip in range(2)
        ]
        absorb(places, pieces, rows, limits, None, (peak, total, summed))
        return 0

    lax.fori_loop(0, (count + 1) // 2, one_pair, 0)
    for g in range(HEADS):
        for chunk in range(CHUNKS):
            where = slice(chunk * TOK, (chunk + 1) * TOK)
            value = summed[g, :, where] / jnp.sum(total[g, :, where], axis=0, keepdims=True)
            column = (g * GROUP + chunk % GROUP) * HD
            out[chunk // GROUP, :, column : column + HD] = jnp.transpose(value.astype(jnp.bfloat16))


def attend_pages(requests, segments, query_seg, rows, state, mine, theirs):
    return pl.pallas_call(
        attend_pages_kernel,
        name="attend_pages",
        out_shape=bf16(LAYERS, TOK, HEADS * GROUP * HD),
        in_specs=[SMEM, SMEM] + [VMEM] * 7,
        out_specs=VMEM,
        scratch_shapes=[
            pltpu.VMEM((HEADS, 8, ROWS), jnp.float32),
            pltpu.VMEM((HEADS, 8, ROWS), jnp.float32),
            pltpu.VMEM((HEADS, HD, ROWS), jnp.float32),
            pltpu.SMEM((HITS + 1,), jnp.int32),
        ],
        compiler_params=params(),
        cost_estimate=cost(3 * 10**9, 6 * 2**20, 5 * 10**6),
    )(requests, segments, query_seg, rows, *state, mine, theirs)


def seq_gather(block, *after):
    mine = relay(
        [
            block,
            lax.ppermute(block, "seq", XDOWN),
            lax.ppermute(block, "seq", XFAR),
            lax.ppermute(block, "seq", XUP),
        ],
        after,
    )
    return mine, lax.ppermute(mine, "seq", CORE)


def on_device(hidden, kv_weight, queries, kv_pool, hit_host, hit_page, hit_request, segment_ids):
    seq = lax.axis_index("seq")
    quarter = lax.rem(seq, 4)
    segments = segment_ids[0]
    query_seg = lax.dynamic_slice_in_dim(segments, seq * TOK, TOK).reshape(1, TOK)

    own_cols = lax.dynamic_slice_in_dim(kv_weight, quarter * HD, HD, 2).reshape(256, 2 * HD)
    near_cols = lax.ppermute(own_cols, "cache", CACHE_NEAR)
    hosts = hit_host[:, :, 0]
    pool = lax.dynamic_slice(
        kv_pool, (0, (seq // 4) * HALF, 0, quarter * HD), (kv_pool.shape[0], HALF, 2, HD)
    ).reshape(kv_pool.shape[0], HALF, 2 * HD)
    sent = stage(hidden[0], pool)
    both = order(own_cols, near_cols, hosts, pool)
    ups, downs = [both], [both]
    for step in range(3):
        ups.append(lax.ppermute(ups[-1], "cache", CACHE_UP))
        downs.append(lax.ppermute(downs[-1], "cache", CACHE_DOWN))
    weights = [both, ups[1], downs[1], ups[2], downs[2], ups[3], downs[3]]

    across = lax.ppermute(hidden[0], "seq", XPAIR)
    other = lax.ppermute(sent, "head", HEAD)
    diagonal = lax.ppermute(sent, ("seq", "head"), DIAGONAL)
    packed = pack(hosts, hit_page, pool, ups[1])
    hidden_mine, half_up, half_down = bundle([sent, across, other, diagonal], ups[3], downs[3], packed)
    far_a = lax.ppermute(half_up, "cache", CACHE_UP)
    far_b = lax.ppermute(half_down, "cache", CACHE_DOWN)
    hidden_theirs = lax.ppermute(hidden_mine, "seq", CORE)

    partial, far_hidden = project_near(hidden_mine, hidden_theirs, weights)
    block = project_far(partial, far_hidden, far_a, far_b)
    arrived = lax.all_to_all(hold(packed, block), "cache", split_axis=0, concat_axis=0, tiled=True)
    new_mine, new_theirs = seq_gather(block)
    rows, bias = prepare(queries[:, 0], query_seg, segments.reshape(8, TOK), new_mine)

    prefix = unpack(hosts, arrived, new_theirs)
    own, *state = attend_new(segments, rows, bias, new_mine, new_theirs, prefix)
    page_mine, page_theirs = seq_gather(prefix, state[0])
    attended = attend_pages(hit_request, segments, query_seg, rows, state, page_mine, page_theirs)
    return attended[:, None], own[None]


def solution(mesh):
    return jax.shard_map(
        on_device,
        mesh=mesh,
        in_specs=(
            P("cache", "seq", "head"),
            P("cache", None, "head"),
            P(None, "cache", "seq", "head"),
            P("cache", None, None, "head"),
            P(),
            P(),
            P(),
            P("cache", None),
        ),
        out_specs=(P(None, "cache", "seq", "head"), P("cache", "seq", None, "head")),
        check_vma=False,
    )
```
